32 devices in a mesh: seq: 16 (over z, y, x), tp: 2 (over core).
Axes of the slice: x: 2, y: 2, z: 4, core: 2. Of those that a mesh axis runs over, the one named last changes fastest.
Arguments:
- queries: bfloat16 [4096, 4096], P('seq', 'tp'), may hold values from -6 to 6
- keys: bfloat16 [4096, 4096], P('seq', 'tp'), may hold values from -6 to 6
- values: bfloat16 [4096, 4096], P('seq', 'tp'), may hold values from -6 to 6
- out_cotangent: bfloat16 [4096, 2048], P('seq', 'tp'), may hold values from -6 to 6
- proj_weight: bfloat16 [4096, 2048], P('tp', 'seq'), may hold values from -0.125 to 0.125
Outputs:
- grad_queries: bfloat16 [4096, 4096], P('seq', 'tp')
- grad_keys: bfloat16 [4096, 4096], P('seq', 'tp')
- grad_values: bfloat16 [4096, 4096], P('seq', 'tp')
- grad_proj: float32 [4096, 2048], P('tp', 'seq')
The draws below stay inside these ranges and needn't reach their ends.
All inputs are finite; a program needn't handle non-finite values.
Results may differ from the reference program's by a relative error of at most 0.0058.
Values may be sent and summed in bfloat16 or wider, within the bound.
A program may use at most 128 MiB of HBM per device.

```python
import jax
import jax.numpy as jnp
from jax import lax

H = 32
DH = 128
COLS = 2048
TOK_DEV = 256
TOKENS = 4096
HD = 4096
N_SEQ = 16


def raised(result, rng, source, target, parts, factor):
    def block_of(position):
        return (jnp.arange(result.shape[position]) // (result.shape[position] // parts)).reshape((-1,) + (1,) * (result.ndim - 1 - position))

    near = jax.random.permutation(rng, parts)[block_of(target)]
    other_side = (block_of(target) + parts // 2) % parts
    return jnp.where((block_of(source) == near) | (block_of(source) == other_side), factor * result, result)


def block_scale(key, extent, pieces, low, top_value):
    def one(dim, parts):
        steps = jax.random.uniform(jax.random.fold_in(jax.random.fold_in(key, 6), dim), (parts,), jnp.float32, low / len(pieces), top_value / len(pieces))
        return jnp.repeat(jnp.exp(steps), extent[dim] // parts).reshape((-1,) + (1,) * (len(extent) - dim - 1))

    factor_of = one(*pieces[0])
    for cut in pieces[1:]:
        factor_of = factor_of * one(*cut)
    return factor_of


def normal_values(stream_key, dims, width, bound, shards=(), dtype=jnp.bfloat16):
    array = width * jax.random.normal(stream_key, dims, jnp.float32)
    if shards:
        array = array * block_scale(stream_key, dims, shards, -0.22, 0.18)
    return jnp.clip(array, -bound, bound).astype(dtype)


def heavy_noise(stream_key, dims, width, limit, split, heavy, kind=jnp.bfloat16):
    entries = width * jax.random.normal(stream_key, dims, jnp.float32)
    if split:
        entries = entries * block_scale(stream_key, dims, split, -0.22, 0.18)
    return jnp.clip(raised(entries, jax.random.fold_in(stream_key, 3), *heavy), -limit, limit).astype(kind)


def setup_inputs(seed: int = 0) -> dict:
    seeds = jax.random.split(jax.random.key(seed), 6)
    return {
        "queries": normal_values(seeds[0], (TOKENS, HD), 1.0, 6.0, ((0, 16), (1, 2))),
        "keys": normal_values(seeds[1], (TOKENS, HD), 1.0, 6.0, ((0, 16), (1, 2))),
        "values": normal_values(seeds[2], (TOKENS, HD), 1.0, 6.0, ((0, 16), (1, 2))),
        "out_cotangent": heavy_noise(seeds[3], (TOKENS, COLS), 1.0, 6.0, ((0, 16), (1, 2)), (0, 1, 16, 2.0)),
        "proj_weight": normal_values(seeds[4], (HD, COLS), COLS ** -0.5, 0.125, ((0, 2), (1, 16))),
    }


def reference(queries, keys, values, out_cotangent, proj_weight):
    blocks = N_SEQ
    scale = 1.0 / jnp.sqrt(jnp.float32(DH * TOKENS))
    q_blk = queries.reshape(blocks, TOK_DEV, H, DH)
    k_blk = keys.reshape(blocks, TOK_DEV, H, DH)
    v_blk = values.reshape(blocks, TOK_DEV, H, DH)
    grad_out = jnp.dot(out_cotangent, proj_weight.T, preferred_element_type=jnp.float32).astype(jnp.bfloat16)
    g_blk = grad_out.reshape(blocks, TOK_DEV, H, DH)
    kv_state = jnp.einsum('bthd,bthe->bhde', k_blk.astype(jnp.float32), v_blk.astype(jnp.float32))
    qg_state = jnp.einsum('bthd,bthe->bhde', q_blk.astype(jnp.float32), g_blk.astype(jnp.float32))
    zeros = jnp.zeros((1, H, DH, DH), jnp.float32)
    prior = jnp.concatenate([zeros, jnp.cumsum(kv_state, axis=0)[:-1]], axis=0).astype(jnp.bfloat16)
    rev = jnp.cumsum(qg_state[::-1], axis=0)[::-1]
    later = jnp.concatenate([rev[1:], zeros], axis=0).astype(jnp.bfloat16)
    rows = jnp.arange(TOK_DEV)
    causal = rows[:, None] >= rows[None, :]

    def one_block(items):
        q, k, v, g, pr, la = items
        qf = q.astype(jnp.float32)
        kf = k.astype(jnp.float32)
        vf = v.astype(jnp.float32)
        gf = g.astype(jnp.float32)
        prf = pr.astype(jnp.float32)
        laf = la.astype(jnp.float32)
        attn = jnp.where(causal[None], jnp.einsum('thd,shd->hts', qf, kf), 0.0).astype(jnp.bfloat16).astype(jnp.float32)
        back = jnp.where(causal[None], jnp.einsum('thd,shd->hts', gf, vf), 0.0).astype(jnp.bfloat16).astype(jnp.float32)
        out = scale * (jnp.einsum('hts,she->the', attn, vf) + jnp.einsum('thd,hde->the', qf, prf))
        dq = scale * (jnp.einsum('hts,shd->thd', back, kf) + jnp.einsum('the,hde->thd', gf, prf))
        dk = scale * (jnp.einsum('hts,thd->shd', back, qf) + jnp.einsum('she,hde->shd', vf, laf))
        dv = scale * (jnp.einsum('hts,the->she', attn, gf) + jnp.einsum('shd,hde->she', kf, laf))
        return (out.astype(jnp.bfloat16), dq.astype(jnp.bfloat16), dk.astype(jnp.bfloat16), dv.astype(jnp.bfloat16))
    out, dq, dk, dv = lax.map(one_block, (q_blk, k_blk, v_blk, g_blk, prior, later))
    attn_out = out.reshape(TOKENS, HD)
    grad_proj = jnp.dot(attn_out.T, out_cotangent, preferred_element_type=jnp.float32) / jnp.sqrt(jnp.float32(TOKENS))
    return (dq.reshape(TOKENS, HD), dk.reshape(TOKENS, HD), dv.reshape(TOKENS, HD), grad_proj)
```

```python
import functools

import jax
import jax.numpy as jnp
import numpy as np
from jax import lax
from jax.experimental import pallas as pl
from jax.experimental.pallas import tpu as pltpu
from jax.sharding import PartitionSpec as P

DH = 128
PLANE = 4
PARTS = 2
F32 = jnp.float32
BF16 = jnp.bfloat16


def dot(a, b, ca, cb):
    return lax.dot_general(a, b, (((ca,), (cb,)), ((), ())), preferred_element_type=F32)


def lanes(start, size):
    return pl.ds(pl.multiple_of(start, DH), size)


class Sems:
    def __init__(self, send, recv):
        self.send, self.recv, self.used = send, recv, 0

    def take(self, count):
        first = self.used
        self.used += count
        return first

    def copy(self, i, src, dst, device):
        return pltpu.make_async_remote_copy(
            src_ref=src,
            dst_ref=dst,
            send_sem=self.send.at[i],
            recv_sem=self.recv.at[i],
            device_id=device,
            device_id_type=pl.DeviceIdType.MESH,
        )


N_SEMS = 64


def kernel(
    depth, scale, proj_scale,
    q, k, v, c, w,
    gq, gk, gv, gp,
    csend, cbuf, ct, wall, attn_s, aall, gsend, grecv, gown, gfull, pacc, pbf, precv,
    gkpart, gvpart, st1, rv1, zs1, zr1, ps1, prior, st2, rv2, zs2, zr2, ps2, later, zacc,
    send_sem, recv_sem,
):
    s, t = lax.axis_index("seq"), lax.axis_index("tp")
    p, z = s % PLANE, s // PLANE
    tok, width = q.shape
    heads = width // DH
    hq = heads // PLANE
    half = c.shape[1] // PLANE
    shard = w.shape[1]
    sems = Sems(send_sem, recv_sem)
    started = []

    def peer(j):
        if j == 0:
            return p
        if j == 1:
            return p + 1 - 2 * (p % 2)
        if j == 2:
            return p + 2 - 4 * (p // 2)
        return PLANE - 1 - p

    def plane_dev(j, tt=None):
        return (z * PLANE + peer(j), t if tt is None else tt)

    def z_dev(zz):
        return (zz * PLANE + p, t)

    def up(j):
        return (z + j) % depth

    def down(j):
        return (z + depth - j) % depth

    barrier = pltpu.get_barrier_semaphore()
    greet = [plane_dev(j) for j in range(1, PLANE)]
    greet += [plane_dev(j, 1 - t) for j in range(PLANE)]
    greet += [z_dev(up(j)) for j in range(1, depth)]
    for dev in greet:
        pl.semaphore_signal(barrier, inc=1, device_id=dev, device_id_type=pl.DeviceIdType.MESH)
    pl.semaphore_wait(barrier, len(greet))

    w_first = sems.take(depth)

    def w_copy(j, slot):
        return sems.copy(w_first + j, w, wall.at[:, lanes(slot * shard, shard)], z_dev(up(j)))

    for j in range(1, depth):
        cp = w_copy(j, z)
        cp.start()
        started.append(cp)

    per = half // shard
    for pp in range(PLANE):
        for zl in range(per):
            col = (zl * PLANE + pp) * shard
            csend[pp, :, zl * shard : (zl + 1) * shard] = c[:, col : col + shard]
    c_first = sems.take(2 * PLANE)

    def c_copy(j, d, block, src_t):
        return sems.copy(
            c_first + 2 * j + d,
            csend.at[peer(j)],
            cbuf.at[block, :, lanes(src_t * half, half)],
            plane_dev(j, t if d == 0 else 1 - t),
        )

    def scan_states(a, b, st):
        def one(h, _):
            cols = lanes(h * DH, DH)
            st[h // hq, h % hq] = dot(a[:, cols], b[:, cols], 0, 0).astype(BF16)
            return 0

        lax.fori_loop(0, heads, one, 0)

    def scan_start(st, rv):
        first = sems.take(PLANE)

        def cp(j, slot):
            return sems.copy(first + j, st.at[peer(j)], rv.at[slot], plane_dev(j))

        for j in range(1, PLANE):
            x = cp(j, p)
            x.start()
            started.append(x)
        rv[p] = st[p]
        return cp

    def scan_depth(cp, rv, zs, zr, reverse):
        for j in range(1, PLANE):
            cp(j, peer(j)).wait_recv()
        total = rv[0].astype(F32)
        for pp in range(1, PLANE):
            total = total + rv[pp].astype(F32)
        zs[...] = total.astype(BF16)
        first = sems.take(depth)

        def zcp(j, slot):
            return sems.copy(first + j, zs, zr.at[slot], z_dev(down(j) if reverse else up(j)))

        for j in range(1, depth):
            @pl.when(z - j >= 0 if reverse else z + j < depth)
            def _():
                zcp(j, z).start()
        return zcp

    def scan_spread(zcp, rv, zr, ps, out, reverse):
        zacc[...] = jnp.zeros_like(zacc)
        for j in range(1, depth):
            @pl.when(z + j < depth if reverse else z - j >= 0)
            def _():
                src = up(j) if reverse else down(j)
                zcp(j, src).wait_recv()
                zacc[...] += zr[src].astype(F32)

        def one(i, _):
            run = zacc[i]
            order = range(PLANE)
            for pp in reversed(order) if reverse else order:
                ps[pp, i] = run.astype(BF16)
                run = run + rv[pp, i].astype(F32)
            return 0

        lax.fori_loop(0, hq, one, 0)
        first = sems.take(PLANE)

        def cp(j, slot):
            return sems.copy(first + j, ps.at[peer(j)], out.at[slot], plane_dev(j))

        for j in range(1, PLANE):
            x = cp(j, p)
            x.start()
            started.append(x)
        out[p] = ps[p]
        return cp

    def scan_depth_sent(zcp, reverse):
        for j in range(1, depth):
            @pl.when(z - j >= 0 if reverse else z + j < depth)
            def _():
                zcp(j, z).wait_send()

    scan_states(k, v, st1)
    kv_cp = scan_start(st1, rv1)

    for j in range(PLANE):
        for d in range(2):
            if j or d:
                cp = c_copy(j, d, p, t)
                cp.start()
                started.append(cp)
    cbuf[p, :, lanes(t * half, half)] = csend[p]
    wall[:, lanes(z * shard, shard)] = w[...]

    causal = lax.broadcasted_iota(jnp.int32, (tok, tok), 0) >= lax.broadcasted_iota(
        jnp.int32, (tok, tok), 1
    )

    def attn_head(h, _):
        cols = lanes(h * DH, DH)
        attn_s[h] = jnp.where(causal, dot(q[:, cols], k[:, cols], 1, 1), 0.0).astype(BF16)
        return 0

    lax.fori_loop(0, heads // 2, attn_head, 0)
    kv_z = scan_depth(kv_cp, rv1, zs1, zr1, False)
    lax.fori_loop(heads // 2, heads, attn_head, 0)
    kv_prior = scan_spread(kv_z, rv1, zr1, ps1, prior, False)
    for j in range(PLANE):
        for d in range(2):
            if j or d:
                c_copy(j, d, peer(j), t if d == 0 else 1 - t).wait_recv()
    for pp in range(PLANE):
        ct[:, pp * tok : (pp + 1) * tok] = cbuf[pp].T
    for j in range(1, PLANE):
        kv_prior(j, peer(j)).wait_recv()

    def out_head(h, _):
        cols = lanes(h * DH, DH)
        a = dot(attn_s[h], v[:, cols], 1, 0) + dot(q[:, cols], prior[h // hq, h % hq], 1, 0)
        aall[p, :, cols] = (scale * a).astype(BF16)
        return 0

    piece = width // PARTS
    a_first = sems.take(PARTS * PLANE)

    def a_copy(part, j, block):
        cols = pl.ds(part * piece, piece)
        return sems.copy(
            a_first + part * PLANE + j, aall.at[p, :, cols], aall.at[block, :, cols], plane_dev(j)
        )

    for part in range(PARTS):
        lax.fori_loop(part * heads // PARTS, (part + 1) * heads // PARTS, out_head, 0)
        for j in range(1, PLANE):
            cp = a_copy(part, j, p)
            cp.start()
            started.append(cp)

    for j in range(1, depth):
        w_copy(j, down(j)).wait_recv()
    step = 4 * DH
    g_first = sems.take(PLANE)

    def g_copy(j):
        return sems.copy(g_first + j, gsend.at[j - 1], grecv.at[j - 1], plane_dev(j))

    for j in (3, 1, 2, 0):
        mine = peer(j)

        def g_chunk(i, _):
            cols = lanes(i * step, step)
            rows = pl.ds(pl.multiple_of(i * step, step), step)
            r = dot(cbuf[mine], wall[rows, :], 1, 1)
            if j:
                gsend[j - 1, :, cols] = r.astype(BF16)
            else:
                gown[:, cols] = r
            return 0

        lax.fori_loop(0, width // step, g_chunk, 0)
        if j:
            cp = g_copy(j)
            cp.start()
            started.append(cp)

    p_first = sems.take(PARTS * depth)

    def p_copy(part, j, slot):
        cols = pl.ds(part * piece, piece)
        return sems.copy(
            p_first + part * depth + j,
            pbf.at[up(j), :, cols],
            precv.at[slot, :, cols],
            z_dev(up(j)),
        )

    def p_chunk(i, _):
        cols = lanes(i * step, step)
        r = dot(ct[...], aall[:, :, cols].reshape(PLANE * tok, step), 1, 0)
        r = r.reshape(depth, shard, step)
        pacc[...] = r
        pbf[:, :, cols] = r.astype(BF16)
        gp[:, cols] = pacc[z]
        return 0

    for part in range(PARTS):
        for j in range(1, PLANE):
            a_copy(part, j, peer(j)).wait_recv()
        lax.fori_loop(part * piece // step, (part + 1) * piece // step, p_chunk, 0)
        for j in range(1, depth):
            cp = p_copy(part, j, z)
            cp.start()
            started.append(cp)

    for j in (1, 2, 3):
        g_copy(j).wait_recv()

    def g_sum(i, _):
        cols = lanes(i * step, step)
        r = gown[:, cols]
        for j in range(PLANE - 1):
            r = r + grecv[j, :, cols].astype(F32)
        gfull[:, cols] = r.astype(BF16)
        return 0

    lax.fori_loop(0, width // step, g_sum, 0)
    scan_states(q, gfull, st2)
    qg_cp = scan_start(st2, rv2)

    def inner_head(h, _):
        cols = lanes(h * DH, DH)
        gh = gfull[:, cols]
        back = jnp.where(causal, dot(gh, v[:, cols], 1, 1), 0.0).astype(BF16)
        dq = dot(back, k[:, cols], 1, 0) + dot(gh, prior[h // hq, h % hq], 1, 1)
        gq[:, cols] = (scale * dq).astype(BF16)
        gkpart[:, cols] = dot(back, q[:, cols], 0, 0)
        gvpart[:, cols] = dot(attn_s[h], gh, 0, 0)
        return 0

    lax.fori_loop(0, heads // 2, inner_head, 0)
    qg_z = scan_depth(qg_cp, rv2, zs2, zr2, True)
    lax.fori_loop(heads // 2, heads, inner_head, 0)
    qg_later = scan_spread(qg_z, rv2, zr2, ps2, later, True)

    for part in range(PARTS):
        for j in range(1, depth):
            p_copy(part, j, down(j)).wait_recv()

    def p_sum(i, _):
        cols = lanes(i * step, step)
        r = gp[:, cols]
        for j in range(1, depth):
            r = r + precv[down(j), :, cols].astype(F32)
        gp[:, cols] = r * proj_scale
        return 0

    lax.fori_loop(0, width // step, p_sum, 0)
    for j in range(1, PLANE):
        qg_later(j, peer(j)).wait_recv()

    def last_head(h, _):
        cols = lanes(h * DH, DH)
        la = later[h // hq, h % hq]
        gk[:, cols] = (scale * (gkpart[:, cols] + dot(v[:, cols], la, 1, 1))).astype(BF16)
        gv[:, cols] = (scale * (gvpart[:, cols] + dot(k[:, cols], la, 1, 0))).astype(BF16)
        return 0

    lax.fori_loop(0, heads, last_head, 0)

    for cp in started:
        cp.wait_send()
    scan_depth_sent(kv_z, False)
    scan_depth_sent(qg_z, True)


def fused(n_seq, queries, keys, values, out_cotangent, proj_weight):
    tok, width = queries.shape
    heads = width // DH
    hq = heads // PLANE
    depth = n_seq // PLANE
    half = out_cotangent.shape[1] // PLANE
    shard = proj_weight.shape[1]
    scale = np.float32(1.0) / np.sqrt(np.float32(DH * tok * n_seq))
    proj_scale = np.float32(1.0) / np.sqrt(np.float32(tok * n_seq))
    bf = lambda *dims: pltpu.VMEM(dims, BF16)
    f32 = lambda *dims: pltpu.VMEM(dims, F32)
    scan = [
        bf(PLANE, hq, DH, DH),
        bf(PLANE, hq, DH, DH),
        bf(hq, DH, DH),
        bf(depth, hq, DH, DH),
        bf(PLANE, hq, DH, DH),
        bf(PLANE, hq, DH, DH),
    ]
    vmem = pl.BlockSpec(memory_space=pltpu.VMEM)
    grad = jax.ShapeDtypeStruct((tok, width), BF16)
    gq, gk, gv, gp = pl.pallas_call(
        functools.partial(kernel, depth, scale, proj_scale),
        out_shape=(grad, grad, grad, jax.ShapeDtypeStruct((shard, width), F32)),
        in_specs=[vmem] * 5,
        out_specs=(vmem,) * 4,
        scratch_shapes=[
            bf(PLANE, tok, half),
            bf(PLANE, tok, 2 * half),
            bf(2 * half, PLANE * tok),
            bf(width, 2 * half),
            bf(heads, tok, tok),
            bf(PLANE, tok, width),
            bf(PLANE - 1, tok, width),
            bf(PLANE - 1, tok, width),
            f32(tok, width),
            bf(tok, width),
            f32(depth, shard, 4 * DH),
            bf(depth, shard, width),
            bf(depth, shard, width),
            f32(tok, width),
            f32(tok, width),
            *scan,
            *scan,
            f32(hq, DH, DH),
            pltpu.SemaphoreType.DMA((N_SEMS,)),
            pltpu.SemaphoreType.DMA((N_SEMS,)),
        ],
        compiler_params=pltpu.CompilerParams(
            collective_id=0, has_side_effects=True, vmem_limit_bytes=58 * 1024 * 1024
        ),
    )(queries, keys, values, out_cotangent, proj_weight)
    return gq, gk, gv, gp.T


def entering(part, axis, combine, identity, reverse):
    count = lax.axis_size(axis)
    place = lax.axis_index(axis)
    ahead = count - 1 - place if reverse else place
    gathered = lax.all_gather(part, axis)
    state = jnp.zeros_like(part) + jnp.asarray(identity, part.dtype)

    def one(step, state):
        source = count - 1 - step if reverse else step
        return combine(state, lax.dynamic_index_in_dim(gathered, source, 0, False))

    return lax.fori_loop(0, ahead, one, state)


def add_pair(earlier, later_one):
    return earlier + later_one


def gathered(queries, keys, values, out_cotangent, proj_weight):
    tok = queries.shape[0]
    heads = queries.shape[1] // DH
    seq_count = lax.axis_size("seq")
    scale = 1.0 / jnp.sqrt(jnp.float32(DH * tok * seq_count))
    q_heads = queries.reshape(tok, heads, DH)
    k_heads = keys.reshape(tok, heads, DH)
    v_heads = values.reshape(tok, heads, DH)
    kv_state = jnp.einsum("thd,the->hde", k_heads, v_heads, preferred_element_type=jnp.float32)
    zero_state = jnp.zeros_like(kv_state)
    prior_sum = entering(kv_state, "seq", add_pair, zero_state, False)
    full_cot = lax.all_gather(out_cotangent, "tp", axis=1, tiled=True)
    grad_out = lax.dot_general(
        full_cot,
        lax.all_gather(proj_weight, "seq", axis=1, tiled=True),
        (((1,), (1,)), ((), ())),
        preferred_element_type=jnp.float32,
    ).astype(jnp.bfloat16)
    g_heads = grad_out.reshape(tok, heads, DH)
    qg_state = jnp.einsum("thd,the->hde", q_heads, g_heads, preferred_element_type=jnp.float32)
    later_sum = entering(qg_state, "seq", add_pair, zero_state, True)
    prior = prior_sum.astype(jnp.bfloat16)
    later = later_sum.astype(jnp.bfloat16)
    rows = jnp.arange(tok)
    causal = (rows[:, None] >= rows[None, :])[None]
    attn = jnp.where(
        causal,
        jnp.einsum("thd,shd->hts", q_heads, k_heads, preferred_element_type=jnp.float32),
        0.0,
    ).astype(jnp.bfloat16)
    back = jnp.where(
        causal,
        jnp.einsum("thd,shd->hts", g_heads, v_heads, preferred_element_type=jnp.float32),
        0.0,
    ).astype(jnp.bfloat16)
    attn_out = scale * (
        jnp.einsum("hts,she->the", attn, v_heads, preferred_element_type=jnp.float32)
        + jnp.einsum("thd,hde->the", q_heads, prior, preferred_element_type=jnp.float32)
    )
    grad_q = scale * (
        jnp.einsum("hts,shd->thd", back, k_heads, preferred_element_type=jnp.float32)
        + jnp.einsum("the,hde->thd", g_heads, prior, preferred_element_type=jnp.float32)
    )
    grad_k = scale * (
        jnp.einsum("hts,thd->shd", back, q_heads, preferred_element_type=jnp.float32)
        + jnp.einsum("she,hde->shd", v_heads, later, preferred_element_type=jnp.float32)
    )
    grad_v = scale * (
        jnp.einsum("hts,the->she", attn, g_heads, preferred_element_type=jnp.float32)
        + jnp.einsum("shd,hde->she", k_heads, later, preferred_element_type=jnp.float32)
    )
    out_flat = attn_out.astype(jnp.bfloat16).reshape(tok, heads * DH)
    proj_term = lax.dot_general(
        out_flat, full_cot, (((0,), (0,)), ((), ())), preferred_element_type=jnp.float32
    )
    proj_sum = lax.psum_scatter(proj_term, "seq", scatter_dimension=1, tiled=True)
    grad_proj = proj_sum / jnp.sqrt(jnp.float32(tok * seq_count))
    width = heads * DH
    return (
        grad_q.astype(jnp.bfloat16).reshape(tok, width),
        grad_k.astype(jnp.bfloat16).reshape(tok, width),
        grad_v.astype(jnp.bfloat16).reshape(tok, width),
        grad_proj,
    )


def per_device(n_seq, n_tp, *args):
    width, shard = args[0].shape[1], args[4].shape[1]
    groups = n_seq % (2 * PLANE) == 0 and n_tp == 2
    if groups and shard % DH == 0 and width % (4 * DH * PARTS) == 0:
        return fused(n_seq, *args)
    return gathered(*args)


def solution(mesh):
    return jax.shard_map(
        functools.partial(per_device, mesh.shape["seq"], mesh.shape["tp"]),
        mesh=mesh,
        in_specs=(P("seq", "tp"), P("seq", "tp"), P("seq", "tp"), P("seq", "tp"), P("tp", "seq")),
        out_specs=(P("seq", "tp"), P("seq", "tp"), P("seq", "tp"), P("tp", "seq")),
        check_vma=False,
    )
```

```python
import functools

import jax
import jax.numpy as jnp
import numpy as np
from jax import lax
from jax.experimental import pallas as pl
from jax.experimental.pallas import tpu as pltpu
from jax.sharding import PartitionSpec as P

DH = 128
PLANE = 4
PARTS = 4
F32 = jnp.float32
BF16 = jnp.bfloat16


def dot(a, b, ca, cb):
    return lax.dot_general(a, b, (((ca,), (cb,)), ((), ())), preferred_element_type=F32)


def lanes(start, size):
    return pl.ds(pl.multiple_of(start, DH), size)


class Sems:
    def __init__(self, send, recv):
        self.send, self.recv, self.used = send, recv, 0

    def take(self, count):
        first = self.used
        self.used += count
        return first

    def copy(self, i, src, dst, device):
        return pltpu.make_async_remote_copy(
            src_ref=src,
            dst_ref=dst,
            send_sem=self.send.at[i],
            recv_sem=self.recv.at[i],
            device_id=device,
            device_id_type=pl.DeviceIdType.MESH,
        )


N_SEMS = 128


def kernel(
    depth, scale, proj_scale,
    q, k, v, c, w,
    gq, gk, gv, gp,
    csend, cbuf, ct, wall, attn_s, aall, gs1, gr1, gkeep, gs2, gr2, gfull, pacc, pown, pbf, precv,
    gkpart, gvpart, st1, rv1, zs1, zr1, ps1, prior, st2, rv2, zs2, zr2, ps2, later, zacc,
    send_sem, recv_sem,
):
    s, t = lax.axis_index("seq"), lax.axis_index("tp")
    p, z = s % PLANE, s // PLANE
    tok, width = q.shape
    heads = width // DH
    hq = heads // (2 * PLANE)
    half = c.shape[1] // PLANE
    shard = w.shape[1]
    sems = Sems(send_sem, recv_sem)
    started = []

    def peer(j):
        if j == 0:
            return p
        if j == 1:
            return p + 1 - 2 * (p % 2)
        if j == 2:
            return p + 2 - 4 * (p // 2)
        return PLANE - 1 - p

    def plane_dev(j, tt=None):
        return (z * PLANE + peer(j), t if tt is None else tt)

    def z_dev(zz):
        return (zz * PLANE + p, t)

    def up(j):
        return (z + j) % depth

    def down(j):
        return (z + depth - j) % depth

    barrier = pltpu.get_barrier_semaphore()
    greet = [plane_dev(j) for j in range(1, PLANE)]
    greet += [plane_dev(j, 1 - t) for j in range(PLANE)]
    greet += [z_dev(up(j)) for j in range(1, depth)]
    for dev in greet:
        pl.semaphore_signal(barrier, inc=1, device_id=dev, device_id_type=pl.DeviceIdType.MESH)

    w_first = sems.take(3 * depth)
    w_cuts = (0, width // 4, width // 2, width)

    def w_copy(part, j, slot):
        rows = pl.ds(w_cuts[part], w_cuts[part + 1] - w_cuts[part])
        return sems.copy(
            w_first + part * depth + j,
            w.at[rows, :],
            wall.at[rows, lanes(slot * shard, shard)],
            z_dev(up(j)),
        )

    def w_send(part):
        for j in range(1, depth):
            cp = w_copy(part, j, z)
            cp.start()
            started.append(cp)

    def w_wait(part):
        for j in range(1, depth):
            w_copy(part, j, down(j)).wait_recv()

    per = half // shard
    for pp in range(PLANE):
        for zl in range(per):
            col = (zl * PLANE + pp) * shard
            csend[pp, :, zl * shard : (zl + 1) * shard] = c[:, col : col + shard]
    c_first = sems.take(2 * PLANE)

    def c_copy(j, block):
        return sems.copy(
            c_first + j, csend.at[peer(j)], cbuf.at[block, :, lanes(t * half, half)], plane_dev(j)
        )

    def c_pass(j, src_t):
        there = cbuf.at[peer(j), :, lanes(src_t * half, half)]
        return sems.copy(c_first + PLANE + j, there, there, plane_dev(0, 1 - t))

    def each_head(lo, hi, one):
        group = heads // 4

        def some(i, _):
            for u in range(group):
                one(lo + i * group + u)
            return 0

        lax.fori_loop(0, (hi - lo) // group, some, 0)

    def of_head(h):
        return h // (PLANE * hq), h // hq % PLANE, h % hq

    def scan_states(a, b, st, hi):
        def one(h):
            cols = lanes(h * DH, DH)
            st[h // hq % PLANE, h % hq] = dot(a[:, cols], b[:, cols], 0, 0).astype(BF16)

        each_head(hi * heads // 2, (hi + 1) * heads // 2, one)

    def scan_start(st, rv):
        first = sems.take(PLANE)

        def cp(j, slot):
            return sems.copy(first + j, st.at[peer(j)], rv.at[slot], plane_dev(j))

        for j in range(1, PLANE):
            x = cp(j, p)
            x.start()
            started.append(x)
        rv[p] = st[p]
        return cp

    def scan_depth(cp, rv, zs, zr, reverse):
        for j in range(1, PLANE):
            cp(j, peer(j)).wait_recv()
        total = rv[0].astype(F32)
        for pp in range(1, PLANE):
            total = total + rv[pp].astype(F32)
        zs[...] = total.astype(BF16)
        first = sems.take(depth)

        def zcp(j, slot):
            return sems.copy(first + j, zs, zr.at[slot], z_dev(down(j) if reverse else up(j)))

        for j in range(1, depth):
            @pl.when(z - j >= 0 if reverse else z + j < depth)
            def _():
                zcp(j, z).start()
        return zcp

    def scan_spread(zcp, rv, zr, ps, out, reverse):
        zacc[...] = jnp.zeros_like(zacc)
        for j in range(1, depth):
            @pl.when(z + j < depth if reverse else z - j >= 0)
            def _():
                src = up(j) if reverse else down(j)
                zcp(j, src).wait_recv()
                zacc[...] += zr[src].astype(F32)

        def one(i, _):
            run = zacc[i]
            order = range(PLANE)
            for pp in reversed(order) if reverse else order:
                ps[pp, i] = run.astype(BF16)
                run = run + rv[pp, i].astype(F32)
            return 0

        lax.fori_loop(0, hq, one, 0)
        first = sems.take(PLANE)

        def cp(j, slot):
            return sems.copy(first + j, ps.at[peer(j)], out.at[slot], plane_dev(j))

        for j in range(1, PLANE):
            x = cp(j, p)
            x.start()
            started.append(x)
        out[p] = ps[p]
        return cp

    def scan_depth_sent(zcp, reverse):
        for j in range(1, depth):
            @pl.when(z - j >= 0 if reverse else z + j < depth)
            def _():
                zcp(j, z).wait_send()

    kv_cp, kv_z, kv_prior = {}, {}, {}
    scan_states(k, v, st1.at[0], 0)
    pl.semaphore_wait(barrier, len(greet))
    kv_cp[0] = scan_start(st1.at[0], rv1.at[0])
    w_send(0)
    scan_states(k, v, st1.at[1], 1)
    kv_cp[1] = scan_start(st1.at[1], rv1.at[1])
    cbuf[p, :, lanes(t * half, half)] = csend[p]
    for j in range(1, PLANE):
        cp = c_copy(j, p)
        cp.start()
        started.append(cp)
    cp = c_pass(0, t)
    cp.start()
    started.append(cp)
    wall[:, lanes(z * shard, shard)] = w[...]

    causal = lax.broadcasted_iota(jnp.int32, (tok, tok), 0) >= lax.broadcasted_iota(
        jnp.int32, (tok, tok), 1
    )

    def attn_head(h):
        cols = lanes(h * DH, DH)
        attn_s[h] = jnp.where(causal, dot(q[:, cols], k[:, cols], 1, 1), 0.0).astype(BF16)

    each_head(0, heads // 2, attn_head)
    for hi in range(2):
        kv_z[hi] = scan_depth(kv_cp[hi], rv1.at[hi], zs1.at[hi], zr1.at[hi], False)
    w_send(1)
    w_send(2)
    each_head(heads // 2, heads, attn_head)
    for j in range(1, PLANE):
        c_copy(j, peer(j)).wait_recv()
        cp = c_pass(j, t)
        cp.start()
        started.append(cp)

    def out_head(h):
        cols = lanes(h * DH, DH)
        a = dot(attn_s[h], v[:, cols], 1, 0) + dot(q[:, cols], prior[of_head(h)], 1, 0)
        aall[p, :, cols] = (scale * a).astype(BF16)

    step = width // PARTS
    a_first = sems.take(PARTS * PLANE)

    def a_copy(part, j, block):
        cols = pl.ds(part * step, step)
        return sems.copy(
            a_first + part * PLANE + j, aall.at[p, :, cols], aall.at[block, :, cols], plane_dev(j)
        )

    def a_pass(part, block):
        cols = pl.ds(part * step, step)
        via = 1 + part % 2
        return sems.copy(
            a_first + part * PLANE + 3,
            aall.at[peer(via), :, cols],
            aall.at[block, :, cols],
            plane_dev(3 - via),
        )

    for hi in range(2):
        kv_prior[hi] = scan_spread(
            kv_z[hi], rv1.at[hi], zr1.at[hi], ps1.at[hi], prior.at[hi], False
        )
        for j in range(1, PLANE):
            kv_prior[hi](j, peer(j)).wait_recv()
        for part in (2 * hi, 2 * hi + 1):
            each_head(part * heads // PARTS, (part + 1) * heads // PARTS, out_head)
            for j in (1, 2):
                cp = a_copy(part, j, p)
                cp.start()
                started.append(cp)
    for j in range(PLANE):
        c_pass(j, 1 - t).wait_recv()
    for pp in range(PLANE):
        ct[:, pp * tok : (pp + 1) * tok] = cbuf[pp].T
    for part in range(PARTS):
        via = 1 + part % 2
        a_copy(part, via, peer(via)).wait_recv()
        cp = a_pass(part, peer(via))
        cp.start()
        started.append(cp)

    def g_block(part, block, out):
        rows = pl.ds(part * step, step)
        out[...] = dot(cbuf[block], wall[rows, :], 1, 1).astype(out.dtype)

    g_first = sems.take(3 * PARTS)

    def g_copy1(part, b):
        return sems.copy(
            g_first + 3 * part + b, gs1.at[part, b], gr1.at[part, b], plane_dev(1 + part % 2)
        )

    def g_copy2(part):
        return sems.copy(g_first + 3 * part + 2, gs2.at[part], gr2.at[part], plane_dev(2 - part % 2))

    def g_first_step(hi):
        both = (2 * hi, 2 * hi + 1)
        for b in (1, 0):
            for part in both:
                g_block(part, peer(3 if b else 1 + part % 2), gs1.at[part, b])
                cp = g_copy1(part, b)
                cp.start()
                started.append(cp)
        for b in (1, 0):
            for part in both:
                g_block(part, peer(2 - part % 2) if b else p, gkeep.at[part, b])

    def g_second_step(hi):
        for part in (2 * hi, 2 * hi + 1):
            g_copy1(part, 1).wait_recv()
            gs2[part] = (gkeep[part, 1] + gr1[part, 1].astype(F32)).astype(BF16)
            cp = g_copy2(part)
            cp.start()
            started.append(cp)

    def g_final(hi):
        for part in (2 * hi, 2 * hi + 1):
            g_copy1(part, 0).wait_recv()
            g_copy2(part).wait_recv()
            total = gkeep[part, 0] + gr1[part, 0].astype(F32) + gr2[part].astype(F32)
            gfull[:, part * step : (part + 1) * step] = total.astype(BF16)

    p_first = sems.take(PARTS * depth)

    def p_copy(part, j, slot):
        cols = pl.ds(part * step, step)
        return sems.copy(
            p_first + part * depth + j,
            pbf.at[up(j), :, cols],
            precv.at[slot, :, cols],
            z_dev(up(j)),
        )

    def p_part(part):
        via = 1 + part % 2
        a_copy(part, 3 - via, peer(3 - via)).wait_recv()
        a_pass(part, peer(3)).wait_recv()
        cols = pl.ds(part * step, step)
        r = dot(ct[...], aall[:, :, cols].reshape(PLANE * tok, step), 1, 0)
        r = r.reshape(depth, shard, step)
        pacc[...] = r
        pbf[:, :, cols] = r.astype(BF16)
        pown[:, cols] = pacc[z]
        for j in range(1, depth):
            cp = p_copy(part, j, z)
            cp.start()
            started.append(cp)

    w_wait(0)
    w_wait(1)
    g_first_step(0)
    p_part(0)
    p_part(1)
    g_second_step(0)
    w_wait(2)
    g_first_step(1)
    p_part(2)
    p_part(3)

    qg_cp, qg_z, qg_later = {}, {}, {}
    g_final(0)
    scan_states(q, gfull, st2.at[0], 0)
    qg_cp[0] = scan_start(st2.at[0], rv2.at[0])
    g_second_step(1)

    def inner_head(h):
        cols = lanes(h * DH, DH)
        gh = gfull[:, cols]
        back = jnp.where(causal, dot(gh, v[:, cols], 1, 1), 0.0).astype(BF16)
        dq = dot(back, k[:, cols], 1, 0) + dot(gh, prior[of_head(h)], 1, 1)
        gq[:, cols] = (scale * dq).astype(BF16)
        gkpart[:, cols] = dot(back, q[:, cols], 0, 0)
        gvpart[:, cols] = dot(attn_s[h], gh, 0, 0)

    each_head(0, heads // 2, inner_head)
    qg_z[0] = scan_depth(qg_cp[0], rv2.at[0], zs2.at[0], zr2.at[0], True)
    g_final(1)
    scan_states(q, gfull, st2.at[1], 1)
    qg_cp[1] = scan_start(st2.at[1], rv2.at[1])
    each_head(heads // 2, heads, inner_head)
    qg_z[1] = scan_depth(qg_cp[1], rv2.at[1], zs2.at[1], zr2.at[1], True)
    qg_later[0] = scan_spread(qg_z[0], rv2.at[0], zr2.at[0], ps2.at[0], later.at[0], True)

    for part in range(PARTS):
        for j in range(1, depth):
            p_copy(part, j, down(j)).wait_recv()

    for part in range(PARTS):
        cols = pl.ds(part * step, step)
        r = pown[:, cols]
        for j in range(1, depth):
            r = r + precv[down(j), :, cols].astype(F32)
        gp[cols, :] = (r * proj_scale).T

    def last_head(h):
        cols = lanes(h * DH, DH)
        la = later[of_head(h)]
        gk[:, cols] = (scale * (gkpart[:, cols] + dot(v[:, cols], la, 1, 1))).astype(BF16)
        gv[:, cols] = (scale * (gvpart[:, cols] + dot(k[:, cols], la, 1, 0))).astype(BF16)

    for j in range(1, PLANE):
        qg_later[0](j, peer(j)).wait_recv()
    each_head(0, heads // 2, last_head)
    qg_later[1] = scan_spread(qg_z[1], rv2.at[1], zr2.at[1], ps2.at[1], later.at[1], True)
    for j in range(1, PLANE):
        qg_later[1](j, peer(j)).wait_recv()
    each_head(heads // 2, heads, last_head)

    for cp in started:
        cp.wait_send()
    for hi in range(2):
        scan_depth_sent(kv_z[hi], False)
        scan_depth_sent(qg_z[hi], True)


def fused(n_seq, queries, keys, values, out_cotangent, proj_weight):
    tok, width = queries.shape
    heads = width // DH
    hq = heads // (2 * PLANE)
    depth = n_seq // PLANE
    half = out_cotangent.shape[1] // PLANE
    shard = proj_weight.shape[1]
    scale = np.float32(1.0) / np.sqrt(np.float32(DH * tok * n_seq))
    proj_scale = np.float32(1.0) / np.sqrt(np.float32(tok * n_seq))
    bf = lambda *dims: pltpu.VMEM(dims, BF16)
    f32 = lambda *dims: pltpu.VMEM(dims, F32)
    scan = [
        bf(2, PLANE, hq, DH, DH),
        bf(2, PLANE, hq, DH, DH),
        bf(2, hq, DH, DH),
        bf(2, depth, hq, DH, DH),
        bf(2, PLANE, hq, DH, DH),
        bf(2, PLANE, hq, DH, DH),
    ]
    vmem = pl.BlockSpec(memory_space=pltpu.VMEM)
    grad = jax.ShapeDtypeStruct((tok, width), BF16)
    return pl.pallas_call(
        functools.partial(kernel, depth, scale, proj_scale),
        out_shape=(grad, grad, grad, jax.ShapeDtypeStruct((width, shard), F32)),
        in_specs=[vmem] * 5,
        out_specs=(vmem,) * 4,
        scratch_shapes=[
            bf(PLANE, tok, half),
            bf(PLANE, tok, 2 * half),
            bf(2 * half, PLANE * tok),
            bf(width, 2 * half),
            bf(heads, tok, tok),
            bf(PLANE, tok, width),
            bf(PARTS, 2, tok, width // PARTS),
            bf(PARTS, 2, tok, width // PARTS),
            f32(PARTS, 2, tok, width // PARTS),
            bf(PARTS, tok, width // PARTS),
            bf(PARTS, tok, width // PARTS),
            bf(tok, width),
            f32(depth, shard, width // PARTS),
            f32(shard, width),
            bf(depth, shard, width),
            bf(depth, shard, width),
            f32(tok, width),
            f32(tok, width),
            *scan,
            *scan,
            f32(hq, DH, DH),
            pltpu.SemaphoreType.DMA((N_SEMS,)),
            pltpu.SemaphoreType.DMA((N_SEMS,)),
        ],
        compiler_params=pltpu.CompilerParams(
            collective_id=0, has_side_effects=True, vmem_limit_bytes=58 * 1024 * 1024
        ),
    )(queries, keys, values, out_cotangent, proj_weight)


def entering(part, axis, combine, identity, reverse):
    count = lax.axis_size(axis)
    place = lax.axis_index(axis)
    ahead = count - 1 - place if reverse else place
    gathered = lax.all_gather(part, axis)
    state = jnp.zeros_like(part) + jnp.asarray(identity, part.dtype)

    def one(step, state):
        source = count - 1 - step if reverse else step
        return combine(state, lax.dynamic_index_in_dim(gathered, source, 0, False))

    return lax.fori_loop(0, ahead, one, state)


def add_pair(earlier, later_one):
    return earlier + later_one


def gathered(queries, keys, values, out_cotangent, proj_weight):
    tok = queries.shape[0]
    heads = queries.shape[1] // DH
    seq_count = lax.axis_size("seq")
    scale = 1.0 / jnp.sqrt(jnp.float32(DH * tok * seq_count))
    q_heads = queries.reshape(tok, heads, DH)
    k_heads = keys.reshape(tok, heads, DH)
    v_heads = values.reshape(tok, heads, DH)
    kv_state = jnp.einsum("thd,the->hde", k_heads, v_heads, preferred_element_type=jnp.float32)
    zero_state = jnp.zeros_like(kv_state)
    prior_sum = entering(kv_state, "seq", add_pair, zero_state, False)
    full_cot = lax.all_gather(out_cotangent, "tp", axis=1, tiled=True)
    grad_out = lax.dot_general(
        full_cot,
        lax.all_gather(proj_weight, "seq", axis=1, tiled=True),
        (((1,), (1,)), ((), ())),
        preferred_element_type=jnp.float32,
    ).astype(jnp.bfloat16)
    g_heads = grad_out.reshape(tok, heads, DH)
    qg_state = jnp.einsum("thd,the->hde", q_heads, g_heads, preferred_element_type=jnp.float32)
    later_sum = entering(qg_state, "seq", add_pair, zero_state, True)
    prior = prior_sum.astype(jnp.bfloat16)
    later = later_sum.astype(jnp.bfloat16)
    rows = jnp.arange(tok)
    causal = (rows[:, None] >= rows[None, :])[None]
    attn = jnp.where(
        causal,
        jnp.einsum("thd,shd->hts", q_heads, k_heads, preferred_element_type=jnp.float32),
        0.0,
    ).astype(jnp.bfloat16)
    back = jnp.where(
        causal,
        jnp.einsum("thd,shd->hts", g_heads, v_heads, preferred_element_type=jnp.float32),
        0.0,
    ).astype(jnp.bfloat16)
    attn_out = scale * (
        jnp.einsum("hts,she->the", attn, v_heads, preferred_element_type=jnp.float32)
        + jnp.einsum("thd,hde->the", q_heads, prior, preferred_element_type=jnp.float32)
    )
    grad_q = scale * (
        jnp.einsum("hts,shd->thd", back, k_heads, preferred_element_type=jnp.float32)
        + jnp.einsum("the,hde->thd", g_heads, prior, preferred_element_type=jnp.float32)
    )
    grad_k = scale * (
        jnp.einsum("hts,thd->shd", back, q_heads, preferred_element_type=jnp.float32)
        + jnp.einsum("she,hde->shd", v_heads, later, preferred_element_type=jnp.float32)
    )
    grad_v = scale * (
        jnp.einsum("hts,the->she", attn, g_heads, preferred_element_type=jnp.float32)
        + jnp.einsum("shd,hde->she", k_heads, later, preferred_element_type=jnp.float32)
    )
    out_flat = attn_out.astype(jnp.bfloat16).reshape(tok, heads * DH)
    proj_term = lax.dot_general(
        out_flat, full_cot, (((0,), (0,)), ((), ())), preferred_element_type=jnp.float32
    )
    proj_sum = lax.psum_scatter(proj_term, "seq", scatter_dimension=1, tiled=True)
    grad_proj = proj_sum / jnp.sqrt(jnp.float32(tok * seq_count))
    width = heads * DH
    return (
        grad_q.astype(jnp.bfloat16).reshape(tok, width),
        grad_k.astype(jnp.bfloat16).reshape(tok, width),
        grad_v.astype(jnp.bfloat16).reshape(tok, width),
        grad_proj,
    )


def per_device(n_seq, n_tp, *args):
    width, shard = args[0].shape[1], args[4].shape[1]
    groups = n_seq % (2 * PLANE) == 0 and n_tp == 2
    if groups and shard % DH == 0 and width % (2 * PLANE * DH) == 0:
        return fused(n_seq, *args)
    return gathered(*args)


def solution(mesh):
    return jax.shard_map(
        functools.partial(per_device, mesh.shape["seq"], mesh.shape["tp"]),
        mesh=mesh,
        in_specs=(P("seq", "tp"), P("seq", "tp"), P("seq", "tp"), P("seq", "tp"), P("tp", "seq")),
        out_specs=(P("seq", "tp"), P("seq", "tp"), P("seq", "tp"), P("tp", "seq")),
        check_vma=False,
    )
```

```python
import functools

import jax
import jax.numpy as jnp
import numpy as np
from jax import lax
from jax.experimental import pallas as pl
from jax.experimental.pallas import tpu as pltpu
from jax.sharding import PartitionSpec as P

DH = 128
PLANE = 4
PARTS = 4
F32 = jnp.float32
BF16 = jnp.bfloat16


def dot(a, b, ca, cb):
    return lax.dot_general(a, b, (((ca,), (cb,)), ((), ())), preferred_element_type=F32)


def lanes(start, size):
    return pl.ds(pl.multiple_of(start, DH), size)


class Sems:
    def __init__(self, send, recv):
        self.send, self.recv, self.used = send, recv, 0

    def take(self, count):
        first = self.used
        self.used += count
        return first

    def copy(self, i, src, dst, device):
        return pltpu.make_async_remote_copy(
            src_ref=src,
            dst_ref=dst,
            send_sem=self.send.at[i],
            recv_sem=self.recv.at[i],
            device_id=device,
            device_id_type=pl.DeviceIdType.MESH,
        )


N_SEMS = 128


def kernel(
    depth, scale, proj_scale,
    q, k, v, c, w,
    gq, gk, gv, gp,
    csend, cbuf, ct, wall, attn_s, aall, gs1, gr1, gkeep, gs2, gr2, gfull, pacc, pbf, prel, psum, precv,
    gkpart, gvpart, st1, rv1, zs1, zr1, ps1, prior, st2, rv2, zs2, zr2, ps2, later, zacc,
    send_sem, recv_sem,
):
    s, t = lax.axis_index("seq"), lax.axis_index("tp")
    p, z = s % PLANE, s // PLANE
    tok, width = q.shape
    heads = width // DH
    hq = heads // (2 * PLANE)
    half = c.shape[1] // PLANE
    shard = w.shape[1]
    sems = Sems(send_sem, recv_sem)
    started = []

    def peer(j):
        if j == 0:
            return p
        if j == 1:
            return p + 1 - 2 * (p % 2)
        if j == 2:
            return p + 2 - 4 * (p // 2)
        return PLANE - 1 - p

    def plane_dev(j, tt=None):
        return (z * PLANE + peer(j), t if tt is None else tt)

    def z_dev(zz):
        return (zz * PLANE + p, t)

    pair = z // 2
    mate = z + 1 - 2 * (z % 2)
    far_in, far_out = 2 - pair, 3 - 3 * pair
    inner, outer = z == 1 + pair, z == 3 * pair

    def up(j):
        return (z + j) % depth

    def down(j):
        return (z + depth - j) % depth

    barrier = pltpu.get_barrier_semaphore()
    greet = [plane_dev(j) for j in range(1, PLANE)]
    greet += [plane_dev(j, 1 - t) for j in range(PLANE)]
    greet += [z_dev(up(j)) for j in range(1, depth)]
    for dev in greet:
        pl.semaphore_signal(barrier, inc=1, device_id=dev, device_id_type=pl.DeviceIdType.MESH)

    w_first = sems.take(15)
    w_cuts = (0, width // 4, width // 2, width)

    def w_copy(part, i, owner, slot, to):
        rows = pl.ds(w_cuts[part], w_cuts[part + 1] - w_cuts[part])
        there = wall.at[rows, lanes(slot * shard, shard)]
        src = w.at[rows, :] if owner is None else wall.at[rows, lanes(owner * shard, shard)]
        return sems.copy(w_first + 5 * part + i, src, there, z_dev(to))

    def w_own(part, slot):
        return w_copy(part, 0, None, slot, mate)

    def w_far(part, i, slot):
        return w_copy(part, 1 + i, None, slot, far_in)

    def w_pass(part, i, owner, slot):
        return w_copy(part, 3 + i, owner, slot, mate)

    def w_send(part):
        for i, mine in enumerate((inner, outer)):
            @pl.when(mine)
            def _():
                w_far(part, i, z).start()
        cp = w_own(part, z)
        cp.start()
        started.append(cp)

    def w_relay(part):
        @pl.when(inner)
        def _():
            for i, owner in enumerate((far_in, far_out)):
                w_far(part, i, owner).wait_recv()
                w_pass(part, i, owner, owner).start()

    def w_wait(part):
        w_own(part, mate).wait_recv()

        @pl.when(outer)
        def _():
            for i, owner in enumerate((far_in, far_out)):
                w_pass(part, i, owner, owner).wait_recv()

    def w_sent(part):
        for i, mine in enumerate((inner, outer)):
            @pl.when(mine)
            def _():
                w_far(part, i, z).wait_send()

        @pl.when(inner)
        def _():
            for i, owner in enumerate((far_in, far_out)):
                w_pass(part, i, owner, owner).wait_send()

    per = half // shard
    for pp in range(PLANE):
        for zl in range(per):
            col = (zl * PLANE + pp) * shard
            csend[pp, :, zl * shard : (zl + 1) * shard] = c[:, col : col + shard]
    c_first = sems.take(2 * PLANE)

    def c_copy(j, block):
        return sems.copy(
            c_first + j, csend.at[peer(j)], cbuf.at[block, :, lanes(t * half, half)], plane_dev(j)
        )

    def c_pass(j, src_t):
        there = cbuf.at[peer(j), :, lanes(src_t * half, half)]
        return sems.copy(c_first + PLANE + j, there, there, plane_dev(0, 1 - t))

    def each_head(lo, hi, one):
        group = heads // 4

        def some(i, _):
            for u in range(group):
                one(lo + i * group + u)
            return 0

        lax.fori_loop(0, (hi - lo) // group, some, 0)

    def of_head(h):
        return h // (PLANE * hq), h // hq % PLANE, h % hq

    def scan_states(a, b, st, hi):
        def one(h):
            cols = lanes(h * DH, DH)
            st[h // hq % PLANE, h % hq] = dot(a[:, cols], b[:, cols], 0, 0).astype(BF16)

        each_head(hi * heads // 2, (hi + 1) * heads // 2, one)

    def scan_start(st, rv):
        first = sems.take(PLANE)

        def cp(j, slot):
            return sems.copy(first + j, st.at[peer(j)], rv.at[slot], plane_dev(j))

        for j in range(1, PLANE):
            x = cp(j, p)
            x.start()
            started.append(x)
        rv[p] = st[p]
        return cp

    def scan_depth(cp, rv, zs, zr, reverse):
        for j in range(1, PLANE):
            cp(j, peer(j)).wait_recv()
        total = rv[0].astype(F32)
        for pp in range(1, PLANE):
            total = total + rv[pp].astype(F32)
        zs[...] = total.astype(BF16)
        first = sems.take(depth)

        def zcp(j, slot):
            return sems.copy(first + j, zs, zr.at[slot], z_dev(down(j) if reverse else up(j)))

        for j in range(1, depth):
            @pl.when(z - j >= 0 if reverse else z + j < depth)
            def _():
                zcp(j, z).start()
        return zcp

    def scan_spread(zcp, rv, zr, ps, out, reverse):
        zacc[...] = jnp.zeros_like(zacc)
        for j in range(1, depth):
            @pl.when(z + j < depth if reverse else z - j >= 0)
            def _():
                src = up(j) if reverse else down(j)
                zcp(j, src).wait_recv()
                zacc[...] += zr[src].astype(F32)

        def one(i, _):
            run = zacc[i]
            order = range(PLANE)
            for pp in reversed(order) if reverse else order:
                ps[pp, i] = run.astype(BF16)
                run = run + rv[pp, i].astype(F32)
            return 0

        lax.fori_loop(0, hq, one, 0)
        first = sems.take(PLANE)

        def cp(j, slot):
            return sems.copy(first + j, ps.at[peer(j)], out.at[slot], plane_dev(j))

        for j in range(1, PLANE):
            x = cp(j, p)
            x.start()
            started.append(x)
        out[p] = ps[p]
        return cp

    def scan_depth_sent(zcp, reverse):
        for j in range(1, depth):
            @pl.when(z - j >= 0 if reverse else z + j < depth)
            def _():
                zcp(j, z).wait_send()

    kv_cp, kv_z, kv_prior = {}, {}, {}
    scan_states(k, v, st1.at[0], 0)
    pl.semaphore_wait(barrier, len(greet))
    kv_cp[0] = scan_start(st1.at[0], rv1.at[0])
    w_send(0)
    scan_states(k, v, st1.at[1], 1)
    kv_cp[1] = scan_start(st1.at[1], rv1.at[1])
    cbuf[p, :, lanes(t * half, half)] = csend[p]
    for j in range(1, PLANE):
        cp = c_copy(j, p)
        cp.start()
        started.append(cp)
    cp = c_pass(0, t)
    cp.start()
    started.append(cp)
    wall[:, lanes(z * shard, shard)] = w[...]

    causal = lax.broadcasted_iota(jnp.int32, (tok, tok), 0) >= lax.broadcasted_iota(
        jnp.int32, (tok, tok), 1
    )

    def attn_head(h):
        cols = lanes(h * DH, DH)
        attn_s[h] = jnp.where(causal, dot(q[:, cols], k[:, cols], 1, 1), 0.0).astype(BF16)

    each_head(0, heads // 2, attn_head)
    for hi in range(2):
        kv_z[hi] = scan_depth(kv_cp[hi], rv1.at[hi], zs1.at[hi], zr1.at[hi], False)
    w_send(1)
    w_send(2)
    each_head(heads // 2, heads, attn_head)
    for j in range(1, PLANE):
        c_copy(j, peer(j)).wait_recv()
        cp = c_pass(j, t)
        cp.start()
        started.append(cp)
    w_relay(0)

    def out_head(h):
        cols = lanes(h * DH, DH)
        a = dot(attn_s[h], v[:, cols], 1, 0) + dot(q[:, cols], prior[of_head(h)], 1, 0)
        aall[p, :, cols] = (scale * a).astype(BF16)

    step = width // PARTS
    a_first = sems.take(PARTS * PLANE)

    def a_copy(part, j, block):
        cols = pl.ds(part * step, step)
        return sems.copy(
            a_first + part * PLANE + j, aall.at[p, :, cols], aall.at[block, :, cols], plane_dev(j)
        )

    def a_pass(part, block):
        cols = pl.ds(part * step, step)
        via = 1 + part % 2
        return sems.copy(
            a_first + part * PLANE + 3,
            aall.at[peer(via), :, cols],
            aall.at[block, :, cols],
            plane_dev(3 - via),
        )

    for hi in range(2):
        kv_prior[hi] = scan_spread(
            kv_z[hi], rv1.at[hi], zr1.at[hi], ps1.at[hi], prior.at[hi], False
        )
        for j in range(1, PLANE):
            kv_prior[hi](j, peer(j)).wait_recv()
        for part in (2 * hi, 2 * hi + 1):
            each_head(part * heads // PARTS, (part + 1) * heads // PARTS, out_head)
            for j in (1, 2):
                cp = a_copy(part, j, p)
                cp.start()
                started.append(cp)
    for j in range(PLANE):
        c_pass(j, 1 - t).wait_recv()
    for pp in range(PLANE):
        ct[:, pp * tok : (pp + 1) * tok] = cbuf[pp].T
    w_relay(1)
    for part in range(PARTS):
        if part == 2:
            w_relay(2)
        via = 1 + part % 2
        a_copy(part, via, peer(via)).wait_recv()
        cp = a_pass(part, peer(via))
        cp.start()
        started.append(cp)

    def g_block(part, block, out):
        rows = pl.ds(part * step, step)
        out[...] = dot(cbuf[block], wall[rows, :], 1, 1).astype(out.dtype)

    g_first = sems.take(3 * PARTS)

    def g_copy1(part, b):
        return sems.copy(
            g_first + 3 * part + b, gs1.at[part, b], gr1.at[part, b], plane_dev(1 + part % 2)
        )

    def g_copy2(part):
        return sems.copy(g_first + 3 * part + 2, gs2.at[part], gr2.at[part], plane_dev(2 - part % 2))

    def g_first_step(hi):
        both = (2 * hi, 2 * hi + 1)
        for b in (1, 0):
            for part in both:
                g_block(part, peer(3 if b else 1 + part % 2), gs1.at[part, b])
                cp = g_copy1(part, b)
                cp.start()
                started.append(cp)
        for b in (1, 0):
            for part in both:
                g_block(part, peer(2 - part % 2) if b else p, gkeep.at[part, b])

    def g_second_step(hi):
        for part in (2 * hi, 2 * hi + 1):
            g_copy1(part, 1).wait_recv()
            gs2[part] = (gkeep[part, 1] + gr1[part, 1].astype(F32)).astype(BF16)
            cp = g_copy2(part)
            cp.start()
            started.append(cp)

    def g_final(hi):
        for part in (2 * hi, 2 * hi + 1):
            g_copy1(part, 0).wait_recv()
            g_copy2(part).wait_recv()
            total = gkeep[part, 0] + gr1[part, 0].astype(F32) + gr2[part].astype(F32)
            gfull[:, part * step : (part + 1) * step] = total.astype(BF16)

    p_first = sems.take(4 * PARTS)
    far = 2 - 2 * pair

    def p_near(part):
        cols = pl.ds(part * step, step)
        return sems.copy(
            p_first + 4 * part, pbf.at[mate, :, cols], precv.at[0, :, cols], z_dev(mate)
        )

    def p_hand(part):
        cols = pl.ds(part * step, step)
        return sems.copy(
            p_first + 4 * part + 1, pbf.at[pl.ds(far, 2), :, cols], prel.at[:, :, cols], z_dev(mate)
        )

    def p_far(part, i):
        cols = pl.ds(part * step, step)
        block, to = ((pair, far_in), (1 - pair, far_out))[i]
        return sems.copy(
            p_first + 4 * part + 2 + i, psum.at[block, :, cols], precv.at[1, :, cols], z_dev(to)
        )

    def p_part(part):
        via = 1 + part % 2
        a_copy(part, 3 - via, peer(3 - via)).wait_recv()
        a_pass(part, peer(3)).wait_recv()
        cols = pl.ds(part * step, step)
        r = dot(ct[...], aall[:, :, cols].reshape(PLANE * tok, step), 1, 0)
        r = r.reshape(depth, shard, step)
        pacc[:, :, cols] = r
        pbf[:, :, cols] = r.astype(BF16)

        @pl.when(outer)
        def _():
            p_hand(part).start()

        cp = p_near(part)
        cp.start()
        started.append(cp)

    def p_relay(part):
        @pl.when(inner)
        def _():
            cols = pl.ds(part * step, step)
            p_hand(part).wait_recv()
            for i in range(2):
                psum[i, :, cols] = (
                    pacc[far + i, :, cols] + prel[i, :, cols].astype(F32)
                ).astype(BF16)
            for i in range(2):
                p_far(part, i).start()

    def p_done(part):
        p_near(part).wait_recv()
        for i, mine in enumerate((inner, outer)):
            @pl.when(mine)
            def _():
                p_far(part, i).wait_recv()

    def p_sent(part):
        @pl.when(outer)
        def _():
            p_hand(part).wait_send()

        @pl.when(inner)
        def _():
            for i in range(2):
                p_far(part, i).wait_send()

    w_wait(0)
    w_wait(1)
    g_first_step(0)
    p_part(0)
    p_part(1)
    g_second_step(0)
    w_wait(2)
    g_first_step(1)
    p_relay(0)
    p_relay(1)
    p_part(2)
    p_part(3)

    qg_cp, qg_z, qg_later = {}, {}, {}
    g_final(0)
    scan_states(q, gfull, st2.at[0], 0)
    qg_cp[0] = scan_start(st2.at[0], rv2.at[0])
    g_second_step(1)
    p_relay(2)
    p_relay(3)

    def inner_head(h):
        cols = lanes(h * DH, DH)
        gh = gfull[:, cols]
        back = jnp.where(causal, dot(gh, v[:, cols], 1, 1), 0.0).astype(BF16)
        dq = dot(back, k[:, cols], 1, 0) + dot(gh, prior[of_head(h)], 1, 1)
        gq[:, cols] = (scale * dq).astype(BF16)
        gkpart[:, cols] = dot(back, q[:, cols], 0, 0)
        gvpart[:, cols] = dot(attn_s[h], gh, 0, 0)

    each_head(0, heads // 2, inner_head)
    qg_z[0] = scan_depth(qg_cp[0], rv2.at[0], zs2.at[0], zr2.at[0], True)
    g_final(1)
    scan_states(q, gfull, st2.at[1], 1)
    qg_cp[1] = scan_start(st2.at[1], rv2.at[1])
    each_head(heads // 2, heads, inner_head)
    qg_z[1] = scan_depth(qg_cp[1], rv2.at[1], zs2.at[1], zr2.at[1], True)
    qg_later[0] = scan_spread(qg_z[0], rv2.at[0], zr2.at[0], ps2.at[0], later.at[0], True)

    for part in range(PARTS):
        cols = pl.ds(part * step, step)
        p_done(part)
        r = pacc[z, :, cols]
        for i in range(2):
            r = r + precv[i, :, cols].astype(F32)
        gp[cols, :] = (r * proj_scale).T

    def last_head(h):
        cols = lanes(h * DH, DH)
        la = later[of_head(h)]
        gk[:, cols] = (scale * (gkpart[:, cols] + dot(v[:, cols], la, 1, 1))).astype(BF16)
        gv[:, cols] = (scale * (gvpart[:, cols] + dot(k[:, cols], la, 1, 0))).astype(BF16)

    for j in range(1, PLANE):
        qg_later[0](j, peer(j)).wait_recv()
    each_head(0, heads // 2, last_head)
    qg_later[1] = scan_spread(qg_z[1], rv2.at[1], zr2.at[1], ps2.at[1], later.at[1], True)
    for j in range(1, PLANE):
        qg_later[1](j, peer(j)).wait_recv()
    each_head(heads // 2, heads, last_head)

    for cp in started:
        cp.wait_send()
    for part in range(3):
        w_sent(part)
    for part in range(PARTS):
        p_sent(part)
    for hi in range(2):
        scan_depth_sent(kv_z[hi], False)
        scan_depth_sent(qg_z[hi], True)


def write_out(*arrays):
    steps = 4

    def body(*refs):
        for src, dst in zip(refs[: len(arrays)], refs[len(arrays) :]):
            dst[...] = src[...]

    specs = [pl.BlockSpec((a.shape[0] // steps, a.shape[1]), lambda i: (i, 0)) for a in arrays]
    return pl.pallas_call(
        body,
        grid=(steps,),
        out_shape=tuple(jax.ShapeDtypeStruct(a.shape, a.dtype) for a in arrays),
        in_specs=specs,
        out_specs=tuple(specs),
    )(*arrays)


def fused(n_seq, queries, keys, values, out_cotangent, proj_weight):
    tok, width = queries.shape
    heads = width // DH
    hq = heads // (2 * PLANE)
    depth = n_seq // PLANE
    half = out_cotangent.shape[1] // PLANE
    shard = proj_weight.shape[1]
    scale = np.float32(1.0) / np.sqrt(np.float32(DH * tok * n_seq))
    proj_scale = np.float32(1.0) / np.sqrt(np.float32(tok * n_seq))
    bf = lambda *dims: pltpu.VMEM(dims, BF16)
    f32 = lambda *dims: pltpu.VMEM(dims, F32)
    scan = [
        bf(2, PLANE, hq, DH, DH),
        bf(2, PLANE, hq, DH, DH),
        bf(2, hq, DH, DH),
        bf(2, depth, hq, DH, DH),
        bf(2, PLANE, hq, DH, DH),
        bf(2, PLANE, hq, DH, DH),
    ]
    vmem = pl.BlockSpec(memory_space=pltpu.VMEM)
    grad = jax.ShapeDtypeStruct((tok, width), BF16)
    outs = pl.pallas_call(
        functools.partial(kernel, depth, scale, proj_scale),
        out_shape=(grad, grad, grad, jax.ShapeDtypeStruct((width, shard), F32)),
        in_specs=[vmem] * 5,
        out_specs=(vmem,) * 4,
        scratch_shapes=[
            bf(PLANE, tok, half),
            bf(PLANE, tok, 2 * half),
            bf(2 * half, PLANE * tok),
            bf(width, 2 * half),
            bf(heads, tok, tok),
            bf(PLANE, tok, width),
            bf(PARTS, 2, tok, width // PARTS),
            bf(PARTS, 2, tok, width // PARTS),
            f32(PARTS, 2, tok, width // PARTS),
            bf(PARTS, tok, width // PARTS),
            bf(PARTS, tok, width // PARTS),
            bf(tok, width),
            f32(depth, shard, width),
            bf(depth, shard, width),
            bf(2, shard, width),
            bf(2, shard, width),
            bf(2, shard, width),
            f32(tok, width),
            f32(tok, width),
            *scan,
            *scan,
            f32(hq, DH, DH),
            pltpu.SemaphoreType.DMA((N_SEMS,)),
            pltpu.SemaphoreType.DMA((N_SEMS,)),
        ],
        compiler_params=pltpu.CompilerParams(
            collective_id=0, has_side_effects=True, vmem_limit_bytes=58 * 1024 * 1024
        ),
    )(queries, keys, values, out_cotangent, proj_weight)
    return write_out(*outs)


def entering(part, axis, combine, identity, reverse):
    count = lax.axis_size(axis)
    place = lax.axis_index(axis)
    ahead = count - 1 - place if reverse else place
    gathered = lax.all_gather(part, axis)
    state = jnp.zeros_like(part) + jnp.asarray(identity, part.dtype)

    def one(step, state):
        source = count - 1 - step if reverse else step
        return combine(state, lax.dynamic_index_in_dim(gathered, source, 0, False))

    return lax.fori_loop(0, ahead, one, state)


def add_pair(earlier, later_one):
    return earlier + later_one


def gathered(queries, keys, values, out_cotangent, proj_weight):
    tok = queries.shape[0]
    heads = queries.shape[1] // DH
    seq_count = lax.axis_size("seq")
    scale = 1.0 / jnp.sqrt(jnp.float32(DH * tok * seq_count))
    q_heads = queries.reshape(tok, heads, DH)
    k_heads = keys.reshape(tok, heads, DH)
    v_heads = values.reshape(tok, heads, DH)
    kv_state = jnp.einsum("thd,the->hde", k_heads, v_heads, preferred_element_type=jnp.float32)
    zero_state = jnp.zeros_like(kv_state)
    prior_sum = entering(kv_state, "seq", add_pair, zero_state, False)
    full_cot = lax.all_gather(out_cotangent, "tp", axis=1, tiled=True)
    grad_out = lax.dot_general(
        full_cot,
        lax.all_gather(proj_weight, "seq", axis=1, tiled=True),
        (((1,), (1,)), ((), ())),
        preferred_element_type=jnp.float32,
    ).astype(jnp.bfloat16)
    g_heads = grad_out.reshape(tok, heads, DH)
    qg_state = jnp.einsum("thd,the->hde", q_heads, g_heads, preferred_element_type=jnp.float32)
    later_sum = entering(qg_state, "seq", add_pair, zero_state, True)
    prior = prior_sum.astype(jnp.bfloat16)
    later = later_sum.astype(jnp.bfloat16)
    rows = jnp.arange(tok)
    causal = (rows[:, None] >= rows[None, :])[None]
    attn = jnp.where(
        causal,
        jnp.einsum("thd,shd->hts", q_heads, k_heads, preferred_element_type=jnp.float32),
        0.0,
    ).astype(jnp.bfloat16)
    back = jnp.where(
        causal,
        jnp.einsum("thd,shd->hts", g_heads, v_heads, preferred_element_type=jnp.float32),
        0.0,
    ).astype(jnp.bfloat16)
    attn_out = scale * (
        jnp.einsum("hts,she->the", attn, v_heads, preferred_element_type=jnp.float32)
        + jnp.einsum("thd,hde->the", q_heads, prior, preferred_element_type=jnp.float32)
    )
    grad_q = scale * (
        jnp.einsum("hts,shd->thd", back, k_heads, preferred_element_type=jnp.float32)
        + jnp.einsum("the,hde->thd", g_heads, prior, preferred_element_type=jnp.float32)
    )
    grad_k = scale * (
        jnp.einsum("hts,thd->shd", back, q_heads, preferred_element_type=jnp.float32)
        + jnp.einsum("she,hde->shd", v_heads, later, preferred_element_type=jnp.float32)
    )
    grad_v = scale * (
        jnp.einsum("hts,the->she", attn, g_heads, preferred_element_type=jnp.float32)
        + jnp.einsum("shd,hde->she", k_heads, later, preferred_element_type=jnp.float32)
    )
    out_flat = attn_out.astype(jnp.bfloat16).reshape(tok, heads * DH)
    proj_term = lax.dot_general(
        out_flat, full_cot, (((0,), (0,)), ((), ())), preferred_element_type=jnp.float32
    )
    proj_sum = lax.psum_scatter(proj_term, "seq", scatter_dimension=1, tiled=True)
    grad_proj = proj_sum / jnp.sqrt(jnp.float32(tok * seq_count))
    width = heads * DH
    return (
        grad_q.astype(jnp.bfloat16).reshape(tok, width),
        grad_k.astype(jnp.bfloat16).reshape(tok, width),
        grad_v.astype(jnp.bfloat16).reshape(tok, width),
        grad_proj,
    )


def per_device(n_seq, n_tp, *args):
    width, shard = args[0].shape[1], args[4].shape[1]
    groups = n_seq == PLANE * PLANE and n_tp == 2
    if groups and shard % DH == 0 and width % (2 * PLANE * DH) == 0:
        return fused(n_seq, *args)
    return gathered(*args)


def solution(mesh):
    return jax.shard_map(
        functools.partial(per_device, mesh.shape["seq"], mesh.shape["tp"]),
        mesh=mesh,
        in_specs=(P("seq", "tp"), P("seq", "tp"), P("seq", "tp"), P("seq", "tp"), P("tp", "seq")),
        out_specs=(P("seq", "tp"), P("seq", "tp"), P("seq", "tp"), P("tp", "seq")),
        check_vma=False,
    )
```

```python
import functools

import jax
import jax.numpy as jnp
import numpy as np
from jax import lax
from jax.experimental import pallas as pl
from jax.experimental.pallas import tpu as pltpu
from jax.sharding import PartitionSpec as P

DH = 128
PLANE = 4
PARTS = 4
F32 = jnp.float32
BF16 = jnp.bfloat16


def dot(a, b, ca, cb):
    return lax.dot_general(a, b, (((ca,), (cb,)), ((), ())), preferred_element_type=F32)


def lanes(start, size):
    return pl.ds(pl.multiple_of(start, DH), size)


class Sems:
    def __init__(self, send, recv):
        self.send, self.recv, self.used = send, recv, 0

    def take(self, count):
        first = self.used
        self.used += count
        return first

    def copy(self, i, src, dst, device):
        return pltpu.make_async_remote_copy(
            src_ref=src,
            dst_ref=dst,
            send_sem=self.send.at[i],
            recv_sem=self.recv.at[i],
            device_id=device,
            device_id_type=pl.DeviceIdType.MESH,
        )


N_SEMS = 176


def kernel(
    depth, scale, proj_scale,
    q, k, v, c, w,
    gq, gk, gv, gp,
    csend, cbuf, ct, wall, attn_s, aall, gs1, gr1, gkeep, gs2, gr2, gfull, pacc, pbf, prel, psum, precv,
    gkpart, gvpart, st1, rv1, zs1, zr1, ps1, prior, st2, rv2, zs2, zr2, ps2, later, zacc,
    send_sem, recv_sem,
):
    s, t = lax.axis_index("seq"), lax.axis_index("tp")
    p, z = s % PLANE, s // PLANE
    tok, width = q.shape
    heads = width // DH
    hq = heads // (PARTS * PLANE)
    half = c.shape[1] // PLANE
    shard = w.shape[1]
    sems = Sems(send_sem, recv_sem)
    started = []

    def peer(j):
        if j == 0:
            return p
        if j == 1:
            return p + 1 - 2 * (p % 2)
        if j == 2:
            return p + 2 - 4 * (p // 2)
        return PLANE - 1 - p

    def plane_dev(j, tt=None):
        return (z * PLANE + peer(j), t if tt is None else tt)

    def z_dev(zz):
        return (zz * PLANE + p, t)

    pair = z // 2
    mate = z + 1 - 2 * (z % 2)
    far_in, far_out = 2 - pair, 3 - 3 * pair
    inner, outer = z == 1 + pair, z == 3 * pair

    def up(j):
        return (z + j) % depth

    def down(j):
        return (z + depth - j) % depth

    barrier = pltpu.get_barrier_semaphore()
    greet = [plane_dev(j) for j in range(1, PLANE)]
    greet += [plane_dev(j, 1 - t) for j in range(PLANE)]
    greet += [z_dev(up(j)) for j in range(1, depth)]
    for dev in greet:
        pl.semaphore_signal(barrier, inc=1, device_id=dev, device_id_type=pl.DeviceIdType.MESH)

    w_first = sems.take(15)
    w_cuts = (0, width // 4, width // 2, width)

    def w_copy(part, i, owner, slot, to):
        rows = pl.ds(w_cuts[part], w_cuts[part + 1] - w_cuts[part])
        there = wall.at[rows, lanes(slot * shard, shard)]
        src = w.at[rows, :] if owner is None else wall.at[rows, lanes(owner * shard, shard)]
        return sems.copy(w_first + 5 * part + i, src, there, z_dev(to))

    def w_own(part, slot):
        return w_copy(part, 0, None, slot, mate)

    def w_far(part, i, slot):
        return w_copy(part, 1 + i, None, slot, far_in)

    def w_pass(part, i, owner, slot):
        return w_copy(part, 3 + i, owner, slot, mate)

    def w_send(part):
        for i, mine in enumerate((inner, outer)):
            @pl.when(mine)
            def _():
                w_far(part, i, z).start()
        cp = w_own(part, z)
        cp.start()
        started.append(cp)

    def w_relay(part):
        @pl.when(inner)
        def _():
            for i, owner in enumerate((far_in, far_out)):
                w_far(part, i, owner).wait_recv()
                w_pass(part, i, owner, owner).start()

    def w_wait(part):
        w_own(part, mate).wait_recv()

        @pl.when(outer)
        def _():
            for i, owner in enumerate((far_in, far_out)):
                w_pass(part, i, owner, owner).wait_recv()

    def w_sent(part):
        for i, mine in enumerate((inner, outer)):
            @pl.when(mine)
            def _():
                w_far(part, i, z).wait_send()

        @pl.when(inner)
        def _():
            for i, owner in enumerate((far_in, far_out)):
                w_pass(part, i, owner, owner).wait_send()

    per = half // shard
    for pp in range(PLANE):
        for zl in range(per):
            col = (zl * PLANE + pp) * shard
            csend[pp, :, zl * shard : (zl + 1) * shard] = c[:, col : col + shard]
    c_first = sems.take(2 * PLANE)

    def c_copy(j, block):
        return sems.copy(
            c_first + j, csend.at[peer(j)], cbuf.at[block, :, lanes(t * half, half)], plane_dev(j)
        )

    def c_pass(j, src_t):
        there = cbuf.at[peer(j), :, lanes(src_t * half, half)]
        return sems.copy(c_first + PLANE + j, there, there, plane_dev(0, 1 - t))

    def each_head(lo, hi, one):
        group = heads // 4

        def some(i, _):
            for u in range(group):
                one(lo + i * group + u)
            return 0

        lax.fori_loop(0, (hi - lo) // group, some, 0)

    def of_head(h):
        return h // (PLANE * hq), h // hq % PLANE, h % hq

    def scan_states(a, b, st, hi):
        def one(h):
            cols = lanes(h * DH, DH)
            st[h // hq % PLANE, h % hq] = dot(a[:, cols], b[:, cols], 0, 0).astype(BF16)

        each_head(hi * heads // PARTS, (hi + 1) * heads // PARTS, one)

    def scan_start(st, rv):
        first = sems.take(PLANE)

        def cp(j, slot):
            return sems.copy(first + j, st.at[peer(j)], rv.at[slot], plane_dev(j))

        for j in range(1, PLANE):
            x = cp(j, p)
            x.start()
            started.append(x)
        rv[p] = st[p]
        return cp

    def scan_depth(cp, rv, zs, zr, reverse):
        for j in range(1, PLANE):
            cp(j, peer(j)).wait_recv()
        total = rv[0].astype(F32)
        for pp in range(1, PLANE):
            total = total + rv[pp].astype(F32)
        zs[...] = total.astype(BF16)
        first = sems.take(depth)

        def zcp(j, slot):
            return sems.copy(first + j, zs, zr.at[slot], z_dev(down(j) if reverse else up(j)))

        for j in range(1, depth):
            @pl.when(z - j >= 0 if reverse else z + j < depth)
            def _():
                zcp(j, z).start()
        return zcp

    def scan_spread(zcp, rv, zr, ps, out, reverse):
        zacc[...] = jnp.zeros_like(zacc)
        for j in range(1, depth):
            @pl.when(z + j < depth if reverse else z - j >= 0)
            def _():
                src = up(j) if reverse else down(j)
                zcp(j, src).wait_recv()
                zacc[...] += zr[src].astype(F32)

        def one(i, _):
            run = zacc[i]
            order = range(PLANE)
            for pp in reversed(order) if reverse else order:
                ps[pp, i] = run.astype(BF16)
                run = run + rv[pp, i].astype(F32)
            return 0

        lax.fori_loop(0, hq, one, 0)
        first = sems.take(PLANE)

        def cp(j, slot):
            return sems.copy(first + j, ps.at[peer(j)], out.at[slot], plane_dev(j))

        for j in range(1, PLANE):
            x = cp(j, p)
            x.start()
            started.append(x)
        out[p] = ps[p]
        return cp

    def scan_depth_sent(zcp, reverse):
        for j in range(1, depth):
            @pl.when(z - j >= 0 if reverse else z + j < depth)
            def _():
                zcp(j, z).wait_send()

    kv_cp, kv_z, kv_prior = {}, {}, {}
    scan_states(k, v, st1.at[0], 0)
    pl.semaphore_wait(barrier, len(greet))
    kv_cp[0] = scan_start(st1.at[0], rv1.at[0])
    w_send(0)
    for part in range(1, PARTS):
        scan_states(k, v, st1.at[part], part)
        kv_cp[part] = scan_start(st1.at[part], rv1.at[part])
    cbuf[p, :, lanes(t * half, half)] = csend[p]
    for j in range(1, PLANE):
        cp = c_copy(j, p)
        cp.start()
        started.append(cp)
    cp = c_pass(0, t)
    cp.start()
    started.append(cp)
    wall[:, lanes(z * shard, shard)] = w[...]

    causal = lax.broadcasted_iota(jnp.int32, (tok, tok), 0) >= lax.broadcasted_iota(
        jnp.int32, (tok, tok), 1
    )

    def attn_head(h):
        cols = lanes(h * DH, DH)
        attn_s[h] = jnp.where(causal, dot(q[:, cols], k[:, cols], 1, 1), 0.0).astype(BF16)

    def kv_depth(part):
        kv_z[part] = scan_depth(kv_cp[part], rv1.at[part], zs1.at[part], zr1.at[part], False)

    def kv_spread(part):
        kv_prior[part] = scan_spread(
            kv_z[part], rv1.at[part], zr1.at[part], ps1.at[part], prior.at[part], False
        )

    for part in range(PARTS):
        kv_depth(part)
    w_send(1)
    w_send(2)
    each_head(0, heads // 2, attn_head)
    kv_spread(0)
    kv_spread(1)
    each_head(heads // 2, heads, attn_head)
    for j in range(1, PLANE):
        c_copy(j, peer(j)).wait_recv()
        cp = c_pass(j, t)
        cp.start()
        started.append(cp)
    w_relay(0)

    def out_head(h):
        cols = lanes(h * DH, DH)
        a = dot(attn_s[h], v[:, cols], 1, 0) + dot(q[:, cols], prior[of_head(h)], 1, 0)
        aall[p, :, cols] = (scale * a).astype(BF16)

    step = width // PARTS
    a_first = sems.take(PARTS * PLANE)

    def a_copy(part, j, block):
        cols = pl.ds(part * step, step)
        return sems.copy(
            a_first + part * PLANE + j, aall.at[p, :, cols], aall.at[block, :, cols], plane_dev(j)
        )

    def a_pass(part, block):
        cols = pl.ds(part * step, step)
        via = 1 + part % 2
        return sems.copy(
            a_first + part * PLANE + 3,
            aall.at[peer(via), :, cols],
            aall.at[block, :, cols],
            plane_dev(3 - via),
        )

    for part in range(PARTS):
        for j in range(1, PLANE):
            kv_prior[part](j, peer(j)).wait_recv()
        each_head(part * heads // PARTS, (part + 1) * heads // PARTS, out_head)
        for j in (1, 2):
            cp = a_copy(part, j, p)
            cp.start()
            started.append(cp)
        if part + 2 < PARTS:
            kv_spread(part + 2)
    for j in range(PLANE):
        c_pass(j, 1 - t).wait_recv()
    for pp in range(PLANE):
        ct[:, pp * tok : (pp + 1) * tok] = cbuf[pp].T
    w_relay(1)
    for part in range(PARTS):
        if part == 2:
            w_relay(2)
        via = 1 + part % 2
        a_copy(part, via, peer(via)).wait_recv()
        cp = a_pass(part, peer(via))
        cp.start()
        started.append(cp)

    def g_block(part, block, out):
        rows = pl.ds(part * step, step)
        out[...] = dot(cbuf[block], wall[rows, :], 1, 1).astype(out.dtype)

    g_first = sems.take(3 * PARTS)

    def g_copy1(part, b):
        return sems.copy(
            g_first + 3 * part + b, gs1.at[part, b], gr1.at[part, b], plane_dev(1 + part % 2)
        )

    def g_copy2(part):
        return sems.copy(g_first + 3 * part + 2, gs2.at[part], gr2.at[part], plane_dev(2 - part % 2))

    def g_first_step(hi):
        both = (2 * hi, 2 * hi + 1)
        for b in (1, 0):
            for part in both:
                g_block(part, peer(3 if b else 1 + part % 2), gs1.at[part, b])
                cp = g_copy1(part, b)
                cp.start()
                started.append(cp)
        for b in (1, 0):
            for part in both:
                g_block(part, peer(2 - part % 2) if b else p, gkeep.at[part, b])

    def g_second_step(hi):
        for part in (2 * hi, 2 * hi + 1):
            g_copy1(part, 1).wait_recv()
            gs2[part] = (gkeep[part, 1] + gr1[part, 1].astype(F32)).astype(BF16)
            cp = g_copy2(part)
            cp.start()
            started.append(cp)

    def g_final(part):
        g_copy1(part, 0).wait_recv()
        g_copy2(part).wait_recv()
        total = gkeep[part, 0] + gr1[part, 0].astype(F32) + gr2[part].astype(F32)
        gfull[:, part * step : (part + 1) * step] = total.astype(BF16)

    p_first = sems.take(4 * PARTS)
    far = 2 - 2 * pair

    def p_near(part):
        cols = pl.ds(part * step, step)
        return sems.copy(
            p_first + 4 * part, pbf.at[mate, :, cols], precv.at[0, :, cols], z_dev(mate)
        )

    def p_hand(part):
        cols = pl.ds(part * step, step)
        return sems.copy(
            p_first + 4 * part + 1, pbf.at[pl.ds(far, 2), :, cols], prel.at[:, :, cols], z_dev(mate)
        )

    def p_far(part, i):
        cols = pl.ds(part * step, step)
        block, to = ((pair, far_in), (1 - pair, far_out))[i]
        return sems.copy(
            p_first + 4 * part + 2 + i, psum.at[block, :, cols], precv.at[1, :, cols], z_dev(to)
        )

    def p_part(part):
        via = 1 + part % 2
        a_copy(part, 3 - via, peer(3 - via)).wait_recv()
        a_pass(part, peer(3)).wait_recv()
        cols = pl.ds(part * step, step)
        r = dot(ct[...], aall[:, :, cols].reshape(PLANE * tok, step), 1, 0)
        r = r.reshape(depth, shard, step)
        pacc[:, :, cols] = r
        pbf[:, :, cols] = r.astype(BF16)

        @pl.when(outer)
        def _():
            p_hand(part).start()

        cp = p_near(part)
        cp.start()
        started.append(cp)

    def p_relay(part):
        @pl.when(inner)
        def _():
            cols = pl.ds(part * step, step)
            p_hand(part).wait_recv()
            for i in range(2):
                psum[i, :, cols] = (
                    pacc[far + i, :, cols] + prel[i, :, cols].astype(F32)
                ).astype(BF16)
            for i in range(2):
                p_far(part, i).start()

    def p_done(part):
        p_near(part).wait_recv()
        for i, mine in enumerate((inner, outer)):
            @pl.when(mine)
            def _():
                p_far(part, i).wait_recv()

    def p_sent(part):
        @pl.when(outer)
        def _():
            p_hand(part).wait_send()

        @pl.when(inner)
        def _():
            for i in range(2):
                p_far(part, i).wait_send()

    w_wait(0)
    w_wait(1)
    g_first_step(0)
    p_part(0)
    p_part(1)
    g_second_step(0)
    w_wait(2)
    g_first_step(1)
    p_relay(0)
    p_relay(1)
    p_part(2)
    p_part(3)

    qg_cp, qg_z, qg_later = {}, {}, {}
    def qg_start(part):
        g_final(part)
        scan_states(q, gfull, st2.at[part], part)
        qg_cp[part] = scan_start(st2.at[part], rv2.at[part])

    def qg_depth(part):
        qg_z[part] = scan_depth(qg_cp[part], rv2.at[part], zs2.at[part], zr2.at[part], True)

    def qg_spread(part):
        qg_later[part] = scan_spread(
            qg_z[part], rv2.at[part], zr2.at[part], ps2.at[part], later.at[part], True
        )

    qg_start(0)
    qg_start(1)
    g_second_step(1)
    p_relay(2)
    p_relay(3)

    def inner_head(h):
        cols = lanes(h * DH, DH)
        gh = gfull[:, cols]
        back = jnp.where(causal, dot(gh, v[:, cols], 1, 1), 0.0).astype(BF16)
        dq = dot(back, k[:, cols], 1, 0) + dot(gh, prior[of_head(h)], 1, 1)
        gq[:, cols] = (scale * dq).astype(BF16)
        gkpart[:, cols] = dot(back, q[:, cols], 0, 0)
        gvpart[:, cols] = dot(attn_s[h], gh, 0, 0)

    each_head(0, heads // 2, inner_head)
    qg_depth(0)
    qg_depth(1)
    qg_start(2)
    qg_start(3)
    qg_spread(0)
    qg_spread(1)
    qg_depth(2)
    qg_depth(3)
    each_head(heads // 2, heads, inner_head)
    qg_spread(2)
    qg_spread(3)

    for part in range(PARTS):
        cols = pl.ds(part * step, step)
        p_done(part)
        r = pacc[z, :, cols]
        for i in range(2):
            r = r + precv[i, :, cols].astype(F32)
        gp[cols, :] = (r * proj_scale).T

    def last_head(h):
        cols = lanes(h * DH, DH)
        la = later[of_head(h)]
        gk[:, cols] = (scale * (gkpart[:, cols] + dot(v[:, cols], la, 1, 1))).astype(BF16)
        gv[:, cols] = (scale * (gvpart[:, cols] + dot(k[:, cols], la, 1, 0))).astype(BF16)

    for part in range(PARTS):
        for j in range(1, PLANE):
            qg_later[part](j, peer(j)).wait_recv()
        each_head(part * heads // PARTS, (part + 1) * heads // PARTS, last_head)

    for cp in started:
        cp.wait_send()
    for part in range(3):
        w_sent(part)
    for part in range(PARTS):
        p_sent(part)
    for part in range(PARTS):
        scan_depth_sent(kv_z[part], False)
        scan_depth_sent(qg_z[part], True)


def write_out(*arrays):
    cuts = 2

    def body(*refs):
        srcs, dsts, sem = refs[: len(arrays)], refs[len(arrays) : -1], refs[-1]
        copies = []
        for i, (src, dst) in enumerate(zip(srcs, dsts)):
            size = src.shape[0] // cuts
            for c in range(cuts):
                rows = pl.ds(c * size, size)
                copies.append(
                    pltpu.make_async_copy(src.at[rows, :], dst.at[rows, :], sem.at[i * cuts + c])
                )
        for cp in copies:
            cp.start()
        for cp in copies:
            cp.wait()

    any_space = pl.BlockSpec(memory_space=pl.ANY)
    return pl.pallas_call(
        body,
        out_shape=tuple(jax.ShapeDtypeStruct(a.shape, a.dtype) for a in arrays),
        in_specs=[any_space] * len(arrays),
        out_specs=(any_space,) * len(arrays),
        scratch_shapes=[pltpu.SemaphoreType.DMA((cuts * len(arrays),))],
    )(*arrays)


def fused(n_seq, queries, keys, values, out_cotangent, proj_weight):
    tok, width = queries.shape
    heads = width // DH
    hq = heads // (PARTS * PLANE)
    depth = n_seq // PLANE
    half = out_cotangent.shape[1] // PLANE
    shard = proj_weight.shape[1]
    scale = np.float32(1.0) / np.sqrt(np.float32(DH * tok * n_seq))
    proj_scale = np.float32(1.0) / np.sqrt(np.float32(tok * n_seq))
    bf = lambda *dims: pltpu.VMEM(dims, BF16)
    f32 = lambda *dims: pltpu.VMEM(dims, F32)
    scan = [
        bf(PARTS, PLANE, hq, DH, DH),
        bf(PARTS, PLANE, hq, DH, DH),
        bf(PARTS, hq, DH, DH),
        bf(PARTS, depth, hq, DH, DH),
        bf(PARTS, PLANE, hq, DH, DH),
        bf(PARTS, PLANE, hq, DH, DH),
    ]
    vmem = pl.BlockSpec(memory_space=pltpu.VMEM)
    grad = jax.ShapeDtypeStruct((tok, width), BF16)
    outs = pl.pallas_call(
        functools.partial(kernel, depth, scale, proj_scale),
        out_shape=(grad, grad, grad, jax.ShapeDtypeStruct((width, shard), F32)),
        in_specs=[vmem] * 5,
        out_specs=(vmem,) * 4,
        scratch_shapes=[
            bf(PLANE, tok, half),
            bf(PLANE, tok, 2 * half),
            bf(2 * half, PLANE * tok),
            bf(width, 2 * half),
            bf(heads, tok, tok),
            bf(PLANE, tok, width),
            bf(PARTS, 2, tok, width // PARTS),
            bf(PARTS, 2, tok, width // PARTS),
            f32(PARTS, 2, tok, width // PARTS),
            bf(PARTS, tok, width // PARTS),
            bf(PARTS, tok, width // PARTS),
            bf(tok, width),
            f32(depth, shard, width),
            bf(depth, shard, width),
            bf(2, shard, width),
            bf(2, shard, width),
            bf(2, shard, width),
            f32(tok, width),
            f32(tok, width),
            *scan,
            *scan,
            f32(hq, DH, DH),
            pltpu.SemaphoreType.DMA((N_SEMS,)),
            pltpu.SemaphoreType.DMA((N_SEMS,)),
        ],
        compiler_params=pltpu.CompilerParams(
            collective_id=0, has_side_effects=True, vmem_limit_bytes=58 * 1024 * 1024
        ),
    )(queries, keys, values, out_cotangent, proj_weight)
    return write_out(*outs)


def entering(part, axis, combine, identity, reverse):
    count = lax.axis_size(axis)
    place = lax.axis_index(axis)
    ahead = count - 1 - place if reverse else place
    gathered = lax.all_gather(part, axis)
    state = jnp.zeros_like(part) + jnp.asarray(identity, part.dtype)

    def one(step, state):
        source = count - 1 - step if reverse else step
        return combine(state, lax.dynamic_index_in_dim(gathered, source, 0, False))

    return lax.fori_loop(0, ahead, one, state)


def add_pair(earlier, later_one):
    return earlier + later_one


def gathered(queries, keys, values, out_cotangent, proj_weight):
    tok = queries.shape[0]
    heads = queries.shape[1] // DH
    seq_count = lax.axis_size("seq")
    scale = 1.0 / jnp.sqrt(jnp.float32(DH * tok * seq_count))
    q_heads = queries.reshape(tok, heads, DH)
    k_heads = keys.reshape(tok, heads, DH)
    v_heads = values.reshape(tok, heads, DH)
    kv_state = jnp.einsum("thd,the->hde", k_heads, v_heads, preferred_element_type=jnp.float32)
    zero_state = jnp.zeros_like(kv_state)
    prior_sum = entering(kv_state, "seq", add_pair, zero_state, False)
    full_cot = lax.all_gather(out_cotangent, "tp", axis=1, tiled=True)
    grad_out = lax.dot_general(
        full_cot,
        lax.all_gather(proj_weight, "seq", axis=1, tiled=True),
        (((1,), (1,)), ((), ())),
        preferred_element_type=jnp.float32,
    ).astype(jnp.bfloat16)
    g_heads = grad_out.reshape(tok, heads, DH)
    qg_state = jnp.einsum("thd,the->hde", q_heads, g_heads, preferred_element_type=jnp.float32)
    later_sum = entering(qg_state, "seq", add_pair, zero_state, True)
    prior = prior_sum.astype(jnp.bfloat16)
    later = later_sum.astype(jnp.bfloat16)
    rows = jnp.arange(tok)
    causal = (rows[:, None] >= rows[None, :])[None]
    attn = jnp.where(
        causal,
        jnp.einsum("thd,shd->hts", q_heads, k_heads, preferred_element_type=jnp.float32),
        0.0,
    ).astype(jnp.bfloat16)
    back = jnp.where(
        causal,
        jnp.einsum("thd,shd->hts", g_heads, v_heads, preferred_element_type=jnp.float32),
        0.0,
    ).astype(jnp.bfloat16)
    attn_out = scale * (
        jnp.einsum("hts,she->the", attn, v_heads, preferred_element_type=jnp.float32)
        + jnp.einsum("thd,hde->the", q_heads, prior, preferred_element_type=jnp.float32)
    )
    grad_q = scale * (
        jnp.einsum("hts,shd->thd", back, k_heads, preferred_element_type=jnp.float32)
        + jnp.einsum("the,hde->thd", g_heads, prior, preferred_element_type=jnp.float32)
    )
    grad_k = scale * (
        jnp.einsum("hts,thd->shd", back, q_heads, preferred_element_type=jnp.float32)
        + jnp.einsum("she,hde->shd", v_heads, later, preferred_element_type=jnp.float32)
    )
    grad_v = scale * (
        jnp.einsum("hts,the->she", attn, g_heads, preferred_element_type=jnp.float32)
        + jnp.einsum("shd,hde->she", k_heads, later, preferred_element_type=jnp.float32)
    )
    out_flat = attn_out.astype(jnp.bfloat16).reshape(tok, heads * DH)
    proj_term = lax.dot_general(
        out_flat, full_cot, (((0,), (0,)), ((), ())), preferred_element_type=jnp.float32
    )
    proj_sum = lax.psum_scatter(proj_term, "seq", scatter_dimension=1, tiled=True)
    grad_proj = proj_sum / jnp.sqrt(jnp.float32(tok * seq_count))
    width = heads * DH
    return (
        grad_q.astype(jnp.bfloat16).reshape(tok, width),
        grad_k.astype(jnp.bfloat16).reshape(tok, width),
        grad_v.astype(jnp.bfloat16).reshape(tok, width),
        grad_proj,
    )


def per_device(n_seq, n_tp, *args):
    width, shard = args[0].shape[1], args[4].shape[1]
    groups = n_seq == PLANE * PLANE and n_tp == 2
    if groups and shard % DH == 0 and width % (PARTS * PLANE * DH) == 0:
        return fused(n_seq, *args)
    return gathered(*args)


def solution(mesh):
    return jax.shard_map(
        functools.partial(per_device, mesh.shape["seq"], mesh.shape["tp"]),
        mesh=mesh,
        in_specs=(P("seq", "tp"), P("seq", "tp"), P("seq", "tp"), P("seq", "tp"), P("tp", "seq")),
        out_specs=(P("seq", "tp"), P("seq", "tp"), P("seq", "tp"), P("tp", "seq")),
        check_vma=False,
    )
```

```python
import functools

import jax
import jax.numpy as jnp
import numpy as np
from jax import lax
from jax.experimental import pallas as pl
from jax.experimental.pallas import tpu as pltpu
from jax.sharding import PartitionSpec as P

DH = 128
PLANE = 4
PARTS = 4
F32 = jnp.float32
BF16 = jnp.bfloat16


def dot(a, b, ca, cb):
    return lax.dot_general(a, b, (((ca,), (cb,)), ((), ())), preferred_element_type=F32)


def lanes(start, size):
    return pl.ds(pl.multiple_of(start, DH), size)


class Sems:
    def __init__(self, send, recv):
        self.send, self.recv, self.used = send, recv, 0

    def take(self, count):
        first = self.used
        self.used += count
        return first

    def copy(self, i, src, dst, device):
        return pltpu.make_async_remote_copy(
            src_ref=src,
            dst_ref=dst,
            send_sem=self.send.at[i],
            recv_sem=self.recv.at[i],
            device_id=device,
            device_id_type=pl.DeviceIdType.MESH,
        )


N_SEMS = 176


def kernel(
    depth, scale, proj_scale,
    q, k, v, c, w,
    gq, gk, gv, gp,
    csend, cbuf, ct, wall, attn_s, aall, gs1, gr1, gkeep, gs2, gr2, gfull, pacc, pbf, prel, psum, precv,
    gkpart, gvpart, st1, rv1, zs1, zr1, ps1, prior, st2, rv2, zs2, zr2, ps2, later, zacc,
    send_sem, recv_sem,
):
    s, t = lax.axis_index("seq"), lax.axis_index("tp")
    p, z = s % PLANE, s // PLANE
    tok, width = q.shape
    heads = width // DH
    hq = heads // (PARTS * PLANE)
    half = c.shape[1] // PLANE
    shard = w.shape[1]
    sems = Sems(send_sem, recv_sem)
    started = []

    def peer(j):
        if j == 0:
            return p
        if j == 1:
            return p + 1 - 2 * (p % 2)
        if j == 2:
            return p + 2 - 4 * (p // 2)
        return PLANE - 1 - p

    def plane_dev(j, tt=None):
        return (z * PLANE + peer(j), t if tt is None else tt)

    def z_dev(zz):
        return (zz * PLANE + p, t)

    pair = z // 2
    mate = z + 1 - 2 * (z % 2)
    far_in, far_out = 2 - pair, 3 - 3 * pair
    inner, outer = z == 1 + pair, z == 3 * pair

    def up(j):
        return (z + j) % depth

    def down(j):
        return (z + depth - j) % depth

    barrier = pltpu.get_barrier_semaphore()
    greet = [plane_dev(j) for j in range(1, PLANE)]
    greet += [plane_dev(j, 1 - t) for j in range(PLANE)]
    greet += [z_dev(up(j)) for j in range(1, depth)]
    for dev in greet:
        pl.semaphore_signal(barrier, inc=1, device_id=dev, device_id_type=pl.DeviceIdType.MESH)

    w_first = sems.take(15)
    w_cuts = (0, width // 4, width // 2, width)

    def w_copy(part, i, owner, slot, to):
        rows = pl.ds(w_cuts[part], w_cuts[part + 1] - w_cuts[part])
        there = wall.at[rows, lanes(slot * shard, shard)]
        src = w.at[rows, :] if owner is None else wall.at[rows, lanes(owner * shard, shard)]
        return sems.copy(w_first + 5 * part + i, src, there, z_dev(to))

    def w_own(part, slot):
        return w_copy(part, 0, None, slot, mate)

    def w_far(part, i, slot):
        return w_copy(part, 1 + i, None, slot, far_in)

    def w_pass(part, i, owner, slot):
        return w_copy(part, 3 + i, owner, slot, mate)

    def w_send(part):
        for i, mine in enumerate((inner, outer)):
            @pl.when(mine)
            def _():
                w_far(part, i, z).start()
        cp = w_own(part, z)
        cp.start()
        started.append(cp)

    def w_relay(part):
        @pl.when(inner)
        def _():
            for i, owner in enumerate((far_in, far_out)):
                w_far(part, i, owner).wait_recv()
                w_pass(part, i, owner, owner).start()

    def w_wait(part):
        w_own(part, mate).wait_recv()

        @pl.when(outer)
        def _():
            for i, owner in enumerate((far_in, far_out)):
                w_pass(part, i, owner, owner).wait_recv()

    def w_sent(part):
        for i, mine in enumerate((inner, outer)):
            @pl.when(mine)
            def _():
                w_far(part, i, z).wait_send()

        @pl.when(inner)
        def _():
            for i, owner in enumerate((far_in, far_out)):
                w_pass(part, i, owner, owner).wait_send()

    per = half // shard
    for pp in range(PLANE):
        for zl in range(per):
            col = (zl * PLANE + pp) * shard
            csend[pp, :, zl * shard : (zl + 1) * shard] = c[:, col : col + shard]
    c_first = sems.take(2 * PLANE)

    def c_copy(j, block):
        return sems.copy(
            c_first + j, csend.at[peer(j)], cbuf.at[block, :, lanes(t * half, half)], plane_dev(j)
        )

    def c_pass(j, src_t):
        there = cbuf.at[peer(j), :, lanes(src_t * half, half)]
        return sems.copy(c_first + PLANE + j, there, there, plane_dev(0, 1 - t))

    def each_head(lo, hi, one):
        group = heads // 4

        def some(i, _):
            for u in range(group):
                one(lo + i * group + u)
            return 0

        lax.fori_loop(0, (hi - lo) // group, some, 0)

    def of_head(h):
        return h // (PLANE * hq), h // hq % PLANE, h % hq

    def scan_states(a, b, st, hi):
        def one(h):
            cols = lanes(h * DH, DH)
            st[h // hq % PLANE, h % hq] = dot(a[:, cols], b[:, cols], 0, 0).astype(BF16)

        each_head(hi * heads // PARTS, (hi + 1) * heads // PARTS, one)

    def scan_start(st, rv):
        first = sems.take(PLANE)

        def cp(j, slot):
            return sems.copy(first + j, st.at[peer(j)], rv.at[slot], plane_dev(j))

        for j in range(1, PLANE):
            x = cp(j, p)
            x.start()
            started.append(x)
        rv[p] = st[p]
        return cp

    def scan_depth(cp, rv, zs, zr, reverse):
        for j in range(1, PLANE):
            cp(j, peer(j)).wait_recv()
        total = rv[0].astype(F32)
        for pp in range(1, PLANE):
            total = total + rv[pp].astype(F32)
        zs[...] = total.astype(BF16)
        first = sems.take(depth)

        def zcp(j, slot):
            return sems.copy(first + j, zs, zr.at[slot], z_dev(down(j) if reverse else up(j)))

        for j in range(1, depth):
            @pl.when(z - j >= 0 if reverse else z + j < depth)
            def _():
                zcp(j, z).start()
        return zcp

    def scan_spread(zcp, rv, zr, ps, out, reverse):
        zacc[...] = jnp.zeros_like(zacc)
        for j in range(1, depth):
            @pl.when(z + j < depth if reverse else z - j >= 0)
            def _():
                src = up(j) if reverse else down(j)
                zcp(j, src).wait_recv()
                zacc[...] += zr[src].astype(F32)

        def one(i, _):
            run = zacc[i]
            order = range(PLANE)
            for pp in reversed(order) if reverse else order:
                ps[pp, i] = run.astype(BF16)
                run = run + rv[pp, i].astype(F32)
            return 0

        lax.fori_loop(0, hq, one, 0)
        first = sems.take(PLANE)

        def cp(j, slot):
            return sems.copy(first + j, ps.at[peer(j)], out.at[slot], plane_dev(j))

        for j in range(1, PLANE):
            x = cp(j, p)
            x.start()
            started.append(x)
        out[p] = ps[p]
        return cp

    def scan_depth_sent(zcp, reverse):
        for j in range(1, depth):
            @pl.when(z - j >= 0 if reverse else z + j < depth)
            def _():
                zcp(j, z).wait_send()

    kv_cp, kv_z, kv_prior = {}, {}, {}
    scan_states(k, v, st1.at[0], 0)
    pl.semaphore_wait(barrier, len(greet))
    kv_cp[0] = scan_start(st1.at[0], rv1.at[0])
    w_send(0)
    for part in range(1, PARTS):
        scan_states(k, v, st1.at[part], part)
        kv_cp[part] = scan_start(st1.at[part], rv1.at[part])
    cbuf[p, :, lanes(t * half, half)] = csend[p]
    for j in range(1, PLANE):
        cp = c_copy(j, p)
        cp.start()
        started.append(cp)
    cp = c_pass(0, t)
    cp.start()
    started.append(cp)
    wall[:, lanes(z * shard, shard)] = w[...]

    causal = lax.broadcasted_iota(jnp.int32, (tok, tok), 0) >= lax.broadcasted_iota(
        jnp.int32, (tok, tok), 1
    )

    def attn_head(h):
        cols = lanes(h * DH, DH)
        attn_s[h] = jnp.where(causal, dot(q[:, cols], k[:, cols], 1, 1), 0.0).astype(BF16)

    def kv_depth(part):
        kv_z[part] = scan_depth(kv_cp[part], rv1.at[part], zs1.at[part], zr1.at[part], False)

    def kv_spread(part):
        kv_prior[part] = scan_spread(
            kv_z[part], rv1.at[part], zr1.at[part], ps1.at[part], prior.at[part], False
        )

    for part in range(PARTS):
        kv_depth(part)
    w_send(1)
    w_send(2)
    each_head(0, heads // 2, attn_head)
    kv_spread(0)
    kv_spread(1)
    each_head(heads // 2, heads, attn_head)
    for j in range(1, PLANE):
        c_copy(j, peer(j)).wait_recv()
        cp = c_pass(j, t)
        cp.start()
        started.append(cp)
    w_relay(0)

    def out_head(h):
        cols = lanes(h * DH, DH)
        a = dot(attn_s[h], v[:, cols], 1, 0) + dot(q[:, cols], prior[of_head(h)], 1, 0)
        aall[p, :, cols] = (scale * a).astype(BF16)

    step = width // PARTS
    a_first = sems.take(PARTS * PLANE)

    def a_copy(part, j, block):
        cols = pl.ds(part * step, step)
        return sems.copy(
            a_first + part * PLANE + j, aall.at[p, :, cols], aall.at[block, :, cols], plane_dev(j)
        )

    def a_pass(part, block):
        cols = pl.ds(part * step, step)
        via = 1 + part % 2
        return sems.copy(
            a_first + part * PLANE + 3,
            aall.at[peer(via), :, cols],
            aall.at[block, :, cols],
            plane_dev(3 - via),
        )

    for part in range(PARTS):
        for j in range(1, PLANE):
            kv_prior[part](j, peer(j)).wait_recv()
        each_head(part * heads // PARTS, (part + 1) * heads // PARTS, out_head)
        for j in (1, 2):
            cp = a_copy(part, j, p)
            cp.start()
            started.append(cp)
        if part + 2 < PARTS:
            kv_spread(part + 2)
    for j in range(PLANE):
        c_pass(j, 1 - t).wait_recv()
    for pp in range(PLANE):
        ct[:, pp * tok : (pp + 1) * tok] = cbuf[pp].T
    w_relay(1)
    for part in range(PARTS):
        if part == 2:
            w_relay(2)
        via = 1 + part % 2
        a_copy(part, via, peer(via)).wait_recv()
        cp = a_pass(part, peer(via))
        cp.start()
        started.append(cp)

    def g_block(part, block, out):
        rows = pl.ds(part * step, step)
        out[...] = dot(cbuf[block], wall[rows, :], 1, 1).astype(out.dtype)

    g_first = sems.take(3 * PARTS)

    def g_copy1(part, b):
        return sems.copy(
            g_first + 3 * part + b, gs1.at[part, b], gr1.at[part, b], plane_dev(1 + part % 2)
        )

    def g_copy2(part):
        return sems.copy(g_first + 3 * part + 2, gs2.at[part], gr2.at[part], plane_dev(2 - part % 2))

    def g_first_step(hi):
        both = (2 * hi, 2 * hi + 1)
        for b in (1, 0):
            for part in both:
                g_block(part, peer(3 if b else 1 + part % 2), gs1.at[part, b])
                cp = g_copy1(part, b)
                cp.start()
                started.append(cp)
        for b in (1, 0):
            for part in both:
                g_block(part, peer(2 - part % 2) if b else p, gkeep.at[part, b])

    def g_second_step(hi):
        for part in (2 * hi, 2 * hi + 1):
            g_copy1(part, 1).wait_recv()
            gs2[part] = (gkeep[part, 1] + gr1[part, 1].astype(F32)).astype(BF16)
            cp = g_copy2(part)
            cp.start()
            started.append(cp)

    def g_final(part):
        g_copy1(part, 0).wait_recv()
        g_copy2(part).wait_recv()
        total = gkeep[part, 0] + gr1[part, 0].astype(F32) + gr2[part].astype(F32)
        gfull[:, part * step : (part + 1) * step] = total.astype(BF16)

    p_first = sems.take(4 * PARTS)
    far = 2 - 2 * pair

    def p_near(part):
        cols = pl.ds(part * step, step)
        return sems.copy(
            p_first + 4 * part, pbf.at[mate, :, cols], precv.at[0, :, cols], z_dev(mate)
        )

    def p_hand(part):
        cols = pl.ds(part * step, step)
        return sems.copy(
            p_first + 4 * part + 1, pbf.at[pl.ds(far, 2), :, cols], prel.at[:, :, cols], z_dev(mate)
        )

    def p_far(part, i):
        cols = pl.ds(part * step, step)
        block, to = ((pair, far_in), (1 - pair, far_out))[i]
        return sems.copy(
            p_first + 4 * part + 2 + i, psum.at[block, :, cols], precv.at[1, :, cols], z_dev(to)
        )

    def p_part(part):
        via = 1 + part % 2
        a_copy(part, 3 - via, peer(3 - via)).wait_recv()
        a_pass(part, peer(3)).wait_recv()
        cols = pl.ds(part * step, step)
        r = dot(ct[...], aall[:, :, cols].reshape(PLANE * tok, step), 1, 0)
        r = r.reshape(depth, shard, step)
        pacc[:, :, cols] = r
        pbf[:, :, cols] = r.astype(BF16)

        @pl.when(outer)
        def _():
            p_hand(part).start()

        cp = p_near(part)
        cp.start()
        started.append(cp)

    def p_relay(part):
        @pl.when(inner)
        def _():
            cols = pl.ds(part * step, step)
            p_hand(part).wait_recv()
            for i in range(2):
                psum[i, :, cols] = (
                    pacc[far + i, :, cols] + prel[i, :, cols].astype(F32)
                ).astype(BF16)
            for i in range(2):
                p_far(part, i).start()

    def p_done(part):
        p_near(part).wait_recv()
        for i, mine in enumerate((inner, outer)):
            @pl.when(mine)
            def _():
                p_far(part, i).wait_recv()

    def p_sent(part):
        @pl.when(outer)
        def _():
            p_hand(part).wait_send()

        @pl.when(inner)
        def _():
            for i in range(2):
                p_far(part, i).wait_send()

    w_wait(0)
    w_wait(1)
    g_first_step(0)
    p_part(0)
    p_part(1)
    g_second_step(0)
    w_wait(2)
    g_first_step(1)
    p_relay(0)
    p_relay(1)
    p_part(2)
    p_part(3)

    qg_cp, qg_z, qg_later = {}, {}, {}
    def qg_start(part):
        g_final(part)
        scan_states(q, gfull, st2.at[part], part)
        qg_cp[part] = scan_start(st2.at[part], rv2.at[part])

    def qg_depth(part):
        qg_z[part] = scan_depth(qg_cp[part], rv2.at[part], zs2.at[part], zr2.at[part], True)

    def qg_spread(part):
        qg_later[part] = scan_spread(
            qg_z[part], rv2.at[part], zr2.at[part], ps2.at[part], later.at[part], True
        )

    qg_start(0)
    qg_start(1)
    g_second_step(1)
    p_relay(2)
    p_relay(3)

    def inner_head(h):
        cols = lanes(h * DH, DH)
        gh = gfull[:, cols]
        back = jnp.where(causal, dot(gh, v[:, cols], 1, 1), 0.0).astype(BF16)
        dq = dot(back, k[:, cols], 1, 0) + dot(gh, prior[of_head(h)], 1, 1)
        gq[:, cols] = (scale * dq).astype(BF16)
        gkpart[:, cols] = dot(back, q[:, cols], 0, 0)
        gvpart[:, cols] = dot(attn_s[h], gh, 0, 0)

    each_head(0, heads // 2, inner_head)
    qg_depth(0)
    qg_depth(1)
    qg_start(2)
    qg_start(3)
    qg_spread(0)
    qg_spread(1)
    qg_depth(2)
    qg_depth(3)
    each_head(heads // 2, heads, inner_head)
    qg_spread(2)
    qg_spread(3)

    for part in range(PARTS):
        cols = pl.ds(part * step, step)
        p_done(part)
        r = pacc[z, :, cols]
        for i in range(2):
            r = r + precv[i, :, cols].astype(F32)
        gp[cols, :] = (r * proj_scale).T

    def last_head(h):
        cols = lanes(h * DH, DH)
        la = later[of_head(h)]
        gk[:, cols] = (scale * (gkpart[:, cols] + dot(v[:, cols], la, 1, 1))).astype(BF16)
        gv[:, cols] = (scale * (gvpart[:, cols] + dot(k[:, cols], la, 1, 0))).astype(BF16)

    for part in range(PARTS):
        for j in range(1, PLANE):
            qg_later[part](j, peer(j)).wait_recv()
        each_head(part * heads // PARTS, (part + 1) * heads // PARTS, last_head)

    for cp in started:
        cp.wait_send()
    for part in range(3):
        w_sent(part)
    for part in range(PARTS):
        p_sent(part)
    for part in range(PARTS):
        scan_depth_sent(kv_z[part], False)
        scan_depth_sent(qg_z[part], True)


def write_out(*arrays):
    cuts = 2
    count = len(arrays)

    def body(*refs):
        srcs, dsts, held = refs[:count], refs[count : 2 * count], refs[2 * count : 3 * count]
        sem_in, sem_out = refs[3 * count :]
        ins, outs = [], []
        for i in range(count):
            size = srcs[i].shape[0] // cuts
            for c in range(cuts):
                rows, n = pl.ds(c * size, size), i * cuts + c
                here = held[i].at[rows, :]
                ins.append(pltpu.make_async_copy(srcs[i].at[rows, :], here, sem_in.at[n]))
                outs.append(pltpu.make_async_copy(here, dsts[i].at[rows, :], sem_out.at[n]))
        for cp in ins:
            cp.start()
        for arrived, leaving in zip(ins, outs):
            arrived.wait()
            leaving.start()
        for cp in outs:
            cp.wait()

    any_space = pl.BlockSpec(memory_space=pl.ANY)
    return pl.pallas_call(
        body,
        out_shape=tuple(jax.ShapeDtypeStruct(a.shape, a.dtype) for a in arrays),
        in_specs=[any_space] * count,
        out_specs=(any_space,) * count,
        scratch_shapes=[
            *(pltpu.VMEM(a.shape, a.dtype) for a in arrays),
            pltpu.SemaphoreType.DMA((cuts * count,)),
            pltpu.SemaphoreType.DMA((cuts * count,)),
        ],
        compiler_params=pltpu.CompilerParams(vmem_limit_bytes=16 * 1024 * 1024),
    )(*arrays)


def fused(n_seq, queries, keys, values, out_cotangent, proj_weight):
    tok, width = queries.shape
    heads = width // DH
    hq = heads // (PARTS * PLANE)
    depth = n_seq // PLANE
    half = out_cotangent.shape[1] // PLANE
    shard = proj_weight.shape[1]
    scale = np.float32(1.0) / np.sqrt(np.float32(DH * tok * n_seq))
    proj_scale = np.float32(1.0) / np.sqrt(np.float32(tok * n_seq))
    bf = lambda *dims: pltpu.VMEM(dims, BF16)
    f32 = lambda *dims: pltpu.VMEM(dims, F32)
    scan = [
        bf(PARTS, PLANE, hq, DH, DH),
        bf(PARTS, PLANE, hq, DH, DH),
        bf(PARTS, hq, DH, DH),
        bf(PARTS, depth, hq, DH, DH),
        bf(PARTS, PLANE, hq, DH, DH),
        bf(PARTS, PLANE, hq, DH, DH),
    ]
    vmem = pl.BlockSpec(memory_space=pltpu.VMEM)
    grad = jax.ShapeDtypeStruct((tok, width), BF16)
    outs = pl.pallas_call(
        functools.partial(kernel, depth, scale, proj_scale),
        out_shape=(grad, grad, grad, jax.ShapeDtypeStruct((width, shard), F32)),
        in_specs=[vmem] * 5,
        out_specs=(vmem,) * 4,
        scratch_shapes=[
            bf(PLANE, tok, half),
            bf(PLANE, tok, 2 * half),
            bf(2 * half, PLANE * tok),
            bf(width, 2 * half),
            bf(heads, tok, tok),
            bf(PLANE, tok, width),
            bf(PARTS, 2, tok, width // PARTS),
            bf(PARTS, 2, tok, width // PARTS),
            f32(PARTS, 2, tok, width // PARTS),
            bf(PARTS, tok, width // PARTS),
            bf(PARTS, tok, width // PARTS),
            bf(tok, width),
            f32(depth, shard, width),
            bf(depth, shard, width),
            bf(2, shard, width),
            bf(2, shard, width),
            bf(2, shard, width),
            f32(tok, width),
            f32(tok, width),
            *scan,
            *scan,
            f32(hq, DH, DH),
            pltpu.SemaphoreType.DMA((N_SEMS,)),
            pltpu.SemaphoreType.DMA((N_SEMS,)),
        ],
        compiler_params=pltpu.CompilerParams(
            collective_id=0, has_side_effects=True, vmem_limit_bytes=58 * 1024 * 1024
        ),
    )(queries, keys, values, out_cotangent, proj_weight)
    return write_out(*outs)


def entering(part, axis, combine, identity, reverse):
    count = lax.axis_size(axis)
    place = lax.axis_index(axis)
    ahead = count - 1 - place if reverse else place
    gathered = lax.all_gather(part, axis)
    state = jnp.zeros_like(part) + jnp.asarray(identity, part.dtype)

    def one(step, state):
        source = count - 1 - step if reverse else step
        return combine(state, lax.dynamic_index_in_dim(gathered, source, 0, False))

    return lax.fori_loop(0, ahead, one, state)


def add_pair(earlier, later_one):
    return earlier + later_one


def gathered(queries, keys, values, out_cotangent, proj_weight):
    tok = queries.shape[0]
    heads = queries.shape[1] // DH
    seq_count = lax.axis_size("seq")
    scale = 1.0 / jnp.sqrt(jnp.float32(DH * tok * seq_count))
    q_heads = queries.reshape(tok, heads, DH)
    k_heads = keys.reshape(tok, heads, DH)
    v_heads = values.reshape(tok, heads, DH)
    kv_state = jnp.einsum("thd,the->hde", k_heads, v_heads, preferred_element_type=jnp.float32)
    zero_state = jnp.zeros_like(kv_state)
    prior_sum = entering(kv_state, "seq", add_pair, zero_state, False)
    full_cot = lax.all_gather(out_cotangent, "tp", axis=1, tiled=True)
    grad_out = lax.dot_general(
        full_cot,
        lax.all_gather(proj_weight, "seq", axis=1, tiled=True),
        (((1,), (1,)), ((), ())),
        preferred_element_type=jnp.float32,
    ).astype(jnp.bfloat16)
    g_heads = grad_out.reshape(tok, heads, DH)
    qg_state = jnp.einsum("thd,the->hde", q_heads, g_heads, preferred_element_type=jnp.float32)
    later_sum = entering(qg_state, "seq", add_pair, zero_state, True)
    prior = prior_sum.astype(jnp.bfloat16)
    later = later_sum.astype(jnp.bfloat16)
    rows = jnp.arange(tok)
    causal = (rows[:, None] >= rows[None, :])[None]
    attn = jnp.where(
        causal,
        jnp.einsum("thd,shd->hts", q_heads, k_heads, preferred_element_type=jnp.float32),
        0.0,
    ).astype(jnp.bfloat16)
    back = jnp.where(
        causal,
        jnp.einsum("thd,shd->hts", g_heads, v_heads, preferred_element_type=jnp.float32),
        0.0,
    ).astype(jnp.bfloat16)
    attn_out = scale * (
        jnp.einsum("hts,she->the", attn, v_heads, preferred_element_type=jnp.float32)
        + jnp.einsum("thd,hde->the", q_heads, prior, preferred_element_type=jnp.float32)
    )
    grad_q = scale * (
        jnp.einsum("hts,shd->thd", back, k_heads, preferred_element_type=jnp.float32)
        + jnp.einsum("the,hde->thd", g_heads, prior, preferred_element_type=jnp.float32)
    )
    grad_k = scale * (
        jnp.einsum("hts,thd->shd", back, q_heads, preferred_element_type=jnp.float32)
        + jnp.einsum("she,hde->shd", v_heads, later, preferred_element_type=jnp.float32)
    )
    grad_v = scale * (
        jnp.einsum("hts,the->she", attn, g_heads, preferred_element_type=jnp.float32)
        + jnp.einsum("shd,hde->she", k_heads, later, preferred_element_type=jnp.float32)
    )
    out_flat = attn_out.astype(jnp.bfloat16).reshape(tok, heads * DH)
    proj_term = lax.dot_general(
        out_flat, full_cot, (((0,), (0,)), ((), ())), preferred_element_type=jnp.float32
    )
    proj_sum = lax.psum_scatter(proj_term, "seq", scatter_dimension=1, tiled=True)
    grad_proj = proj_sum / jnp.sqrt(jnp.float32(tok * seq_count))
    width = heads * DH
    return (
        grad_q.astype(jnp.bfloat16).reshape(tok, width),
        grad_k.astype(jnp.bfloat16).reshape(tok, width),
        grad_v.astype(jnp.bfloat16).reshape(tok, width),
        grad_proj,
    )


def per_device(n_seq, n_tp, *args):
    width, shard = args[0].shape[1], args[4].shape[1]
    groups = n_seq == PLANE * PLANE and n_tp == 2
    if groups and shard % DH == 0 and width % (PARTS * PLANE * DH) == 0:
        return fused(n_seq, *args)
    return gathered(*args)


def solution(mesh):
    return jax.shard_map(
        functools.partial(per_device, mesh.shape["seq"], mesh.shape["tp"]),
        mesh=mesh,
        in_specs=(P("seq", "tp"), P("seq", "tp"), P("seq", "tp"), P("seq", "tp"), P("tp", "seq")),
        out_specs=(P("seq", "tp"), P("seq", "tp"), P("seq", "tp"), P("tp", "seq")),
        check_vma=False,
    )
```
